32 devices in a mesh: section: 2 (over x), batch: 16 (over z, y, core).
Axes of the slice: x: 2, y: 2, z: 4, core: 2. Of those that a mesh axis runs over, the one named last changes fastest.
Arguments:
- inputs: bfloat16 [9216, 768], P('batch', 'section'), may hold values from -6 to 6
- seq_lengths: int32 [16, 8], P('batch'), may hold values from 0 to 576, as said below
- cotangent: bfloat16 [9216, 768], P('batch', 'section'), may hold values from -6 to 6
- first_gain: float32 [768], replicated, may hold values from 0.25 to 1.75
- first_bias: float32 [768], replicated, may hold values from -2 to 2
- joint_weight: bfloat16 [768, 2304], replicated, may hold values from -0.21875 to 0.21875
- query_bias: float32 [768], replicated, may hold values from -2 to 2
- value_bias: float32 [768], replicated, may hold values from -2 to 2
- second_gain: float32 [768], replicated, may hold values from 0.25 to 1.75
- second_bias: float32 [768], replicated, may hold values from -2 to 2
- output_weight: bfloat16 [768, 768], replicated, may hold values from -0.21875 to 0.21875
- output_bias: float32 [768], replicated, may hold values from -2 to 2
- third_gain: float32 [768], replicated, may hold values from 0.25 to 1.75
- third_bias: float32 [768], replicated, may hold values from -2 to 2
- inner_weight: bfloat16 [768, 3072], replicated, may hold values from -0.21875 to 0.21875
- inner_bias: float32 [3072], replicated, may hold values from -2 to 2
- fourth_gain: float32 [3072], replicated, may hold values from 0.25 to 1.75
- fourth_bias: float32 [3072], replicated, may hold values from -2 to 2
- down_weight: bfloat16 [3072, 768], replicated, may hold values from -0.109375 to 0.109375
- down_bias: float32 [768], replicated, may hold values from -2 to 2
Outputs:
- result: bfloat16 [9216, 768], P('batch', 'section')
- input_grad: bfloat16 [9216, 768], P('batch', 'section')
- first_gain_grad: float32 [768], P('section')
- first_bias_grad: float32 [768], P('section')
- joint_weight_grad: float32 [768, 2304], P('section')
- query_bias_grad: float32 [768], P('section')
- value_bias_grad: float32 [768], P('section')
- second_gain_grad: float32 [768], P('section')
- second_bias_grad: float32 [768], P('section')
- output_weight_grad: float32 [768, 768], P('section')
- output_bias_grad: float32 [768], P('section')
- third_gain_grad: float32 [768], P('section')
- third_bias_grad: float32 [768], P('section')
- inner_weight_grad: float32 [768, 3072], P('section')
- inner_bias_grad: float32 [3072], P('section')
- fourth_gain_grad: float32 [3072], P('section')
- fourth_bias_grad: float32 [3072], P('section')
- down_weight_grad: float32 [3072, 768], P('section')
- down_bias_grad: float32 [768], P('section')
The draws below stay inside these ranges and needn't reach their ends.
Inputs may be any that keep to these rules, and one draw needn't show every extreme that they name: `seq_lengths`: row b lists the lengths of the sequences packed one after another from the first of the 576 token slots of batch index b; a row sums to at most 576, the slots after that sum are padding, and a zero marks an unused sequence slot. In every draw some batch index holds one sequence that fills all 576 slots.
All inputs are finite; a program needn't handle non-finite values.
Results may differ from the reference program's by a relative error of at most 0.012.
Values may be sent and summed in bfloat16 or wider, within the bound.
A program may use at most 192 MiB of HBM per device.

```python
import jax
import jax.numpy as jnp
from jax import lax

D = 768
HEADS = 12
HSIZE = 64
FF = 3072
ROWS = 576
SEQS = 8
QBLOCK = 576
TOKENS = 9216
N_BATCH = 16


def draw_seq_lengths(key, part):
    key = jax.random.fold_in(key, 7)
    key_exponent, key_live, key_full = jax.random.split(key, 3)
    exponent = jax.random.randint(key_exponent, (N_BATCH, SEQS), 0, 7)
    weights = jnp.left_shift(jnp.ones((N_BATCH, SEQS), jnp.int32), exponent)
    filled = jax.random.randint(key_live, (N_BATCH, 1), ROWS // 2, ROWS + 1)
    lengths = weights * filled // jnp.sum(weights, axis=1, keepdims=True)
    full_device = jax.random.randint(key_full, (), 0, N_BATCH)
    device_ids = lax.iota(jnp.int32, N_BATCH)[:, None]
    slot_ids = lax.iota(jnp.int32, SEQS)[None, :]
    whole = jnp.where(slot_ids == 0, ROWS, 0)
    return jnp.where(device_ids == full_device, whole, lengths).astype(jnp.int32)


def block_scale(stream_key, dims, cuts, least, top_value):
    def one(axis_at, shards_of):
        draws = jax.random.uniform(jax.random.fold_in(jax.random.fold_in(stream_key, 6), axis_at), (shards_of,), jnp.float32, least / len(cuts), top_value / len(cuts))
        return jnp.repeat(jnp.exp(draws), dims[axis_at] // shards_of).reshape((-1,) + (1,) * (len(dims) - axis_at - 1))

    level = one(*cuts[0])
    for cut in cuts[1:]:
        level = level * one(*cut)
    return level


def centred(stream_key, extent, deviation, bound, cuts=(), dtype=jnp.bfloat16):
    gain = block_scale(stream_key, extent, cuts, -0.22, 0.18) if cuts else 1.0
    entries = jax.random.normal(stream_key, extent, jnp.float32) * deviation * gain
    return jnp.minimum(jnp.maximum(entries, -bound), bound).astype(dtype)


def setup_inputs(seed: int = 0) -> dict:
    streams_of = jax.random.split(jax.random.key(seed), 21)
    return {
        "inputs": centred(streams_of[0], (TOKENS, D), 1.0, 6.0, ((0, 16), (1, 2))),
        "seq_lengths": draw_seq_lengths(jax.random.fold_in(streams_of[20], 71), 0),
        "cotangent": centred(streams_of[2], (TOKENS, D), 1.0, 6.0, ((0, 16), (1, 2))),
        "first_gain": jnp.clip(1.0 + 0.15 * jax.random.normal(streams_of[3], (D,), jnp.float32), 0.25, 1.75),
        "first_bias": centred(streams_of[4], (D,), 0.3, 2.0, (), jnp.float32),
        "joint_weight": centred(streams_of[5], (D, 3 * D), D ** -0.5, 0.21875),
        "query_bias": centred(streams_of[6], (D,), 0.3, 2.0, (), jnp.float32),
        "value_bias": centred(streams_of[7], (D,), 0.3, 2.0, (), jnp.float32),
        "second_gain": jnp.clip(1.0 + 0.15 * jax.random.normal(streams_of[8], (D,), jnp.float32), 0.25, 1.75),
        "second_bias": centred(streams_of[9], (D,), 0.3, 2.0, (), jnp.float32),
        "output_weight": centred(streams_of[10], (D, D), D ** -0.5, 0.21875),
        "output_bias": centred(streams_of[11], (D,), 0.3, 2.0, (), jnp.float32),
        "third_gain": jnp.clip(1.0 + 0.15 * jax.random.normal(streams_of[12], (D,), jnp.float32), 0.25, 1.75),
        "third_bias": centred(streams_of[13], (D,), 0.3, 2.0, (), jnp.float32),
        "inner_weight": centred(streams_of[14], (D, FF), D ** -0.5, 0.21875),
        "inner_bias": centred(streams_of[15], (FF,), 0.3, 2.0, (), jnp.float32),
        "fourth_gain": jnp.clip(1.0 + 0.15 * jax.random.normal(streams_of[16], (FF,), jnp.float32), 0.25, 1.75),
        "fourth_bias": centred(streams_of[17], (FF,), 0.3, 2.0, (), jnp.float32),
        "down_weight": centred(streams_of[18], (FF, D), FF ** -0.5, 0.109375),
        "down_bias": centred(streams_of[19], (D,), 0.3, 2.0, (), jnp.float32),
    }


EPSILON = 1e-05
MASKED = -1000000000.0
HIGH = lax.Precision.HIGHEST

@jax.custom_vjp
def low(v):
    return lax.optimization_barrier(v.astype(jnp.bfloat16)).astype(jnp.float32)

@jax.custom_vjp
def low_back(v):
    return v

def low_keep(v):
    return (low(v), None)

def low_pass(kept, grad):
    return (grad,)

def back_keep(v):
    return (v, None)

def back_low(kept, grad):
    return (low(grad),)
low.defvjp(low_keep, low_pass)
low_back.defvjp(back_keep, back_low)

def layer_norm(values, norm_gain, norm_bias):
    average = lax.optimization_barrier(jnp.mean(values, axis=-1, keepdims=True))
    centered = values - average
    spread = lax.optimization_barrier(jnp.mean(centered * centered, axis=-1, keepdims=True))
    return centered * lax.rsqrt(spread + EPSILON) * norm_gain + norm_bias

def matmul(left, right):
    return jnp.dot(left, right, precision=HIGH, preferred_element_type=jnp.float32)

def packing(lengths):
    ends_at = jnp.cumsum(lengths).astype(jnp.int32)
    places = lax.iota(jnp.int32, ROWS)
    segment = lax.optimization_barrier(jnp.sum((places[:, None] >= ends_at[None, :]).astype(jnp.int32), axis=1)).astype(jnp.int32)
    live_rows = (places < ends_at[-1]).astype(jnp.float32)[:, None]
    return (places, segment, live_rows)

def sublayers(features, lengths, weights):
    first_gain, first_bias, joint_weight, query_bias, value_bias, second_gain, second_bias, output_weight, output_bias, third_gain, third_bias, inner_weight, inner_bias, fourth_gain, fourth_bias, down_weight, down_bias = weights
    places, segment, live_rows = packing(lengths)
    feature_count = features.shape[1]
    factor = HSIZE ** (-0.5)
    normed = low(layer_norm(features, first_gain, first_bias))
    joined = matmul(normed, joint_weight)
    query_rows = low_back(low(joined[:, :feature_count] + query_bias))
    key_rows = low_back(low(joined[:, feature_count:2 * feature_count]))
    value_rows = low_back(low(joined[:, 2 * feature_count:] + value_bias))
    key_heads = key_rows.reshape(ROWS, HEADS, HSIZE)
    value_heads = value_rows.reshape(ROWS, HEADS, HSIZE)

    def attend_block(first_row):
        query_block = lax.dynamic_slice_in_dim(query_rows, first_row, QBLOCK, 0).reshape(QBLOCK, HEADS, HSIZE)
        raw_scores = jnp.einsum('qhd,khd->hqk', query_block, key_heads, precision=HIGH) * factor
        scores = low_back(raw_scores)
        query_place = lax.dynamic_slice_in_dim(places, first_row, QBLOCK, 0)
        query_segment = lax.dynamic_slice_in_dim(segment, first_row, QBLOCK, 0)
        allowed = (query_segment[:, None] == segment[None, :]) & (places[None, :] <= query_place[:, None])
        scores = jnp.where(allowed[None], scores, MASKED)
        largest = lax.optimization_barrier(jnp.max(scores, axis=2, keepdims=True))
        shifted = jnp.exp(scores - largest)
        soft_weights = low(shifted / lax.optimization_barrier(jnp.sum(shifted, axis=2, keepdims=True)))
        mixed = jnp.einsum('hqk,khd->qhd', soft_weights, value_heads, precision=HIGH)
        return mixed.reshape(QBLOCK, feature_count)
    starts = lax.iota(jnp.int32, ROWS // QBLOCK) * QBLOCK
    mixed_rows = low_back(lax.map(jax.checkpoint(attend_block), starts).reshape(ROWS, feature_count))
    subnormed = low(layer_norm(mixed_rows, second_gain, second_bias))
    branch = low_back(matmul(subnormed, output_weight) + output_bias)
    handed = low_back(low(features + branch))
    feed_normed = low(layer_norm(handed, third_gain, third_bias))
    inner_rows = low_back(matmul(feed_normed, inner_weight) + inner_bias)
    activated = jax.nn.gelu(inner_rows, approximate=True)
    feed_subnorm = low(layer_norm(activated, fourth_gain, fourth_bias))
    feed_branch = low_back(matmul(feed_subnorm, down_weight) + down_bias)
    return live_rows * (handed + feed_branch)

def reference(inputs, seq_lengths, cotangent, first_gain, first_bias, joint_weight, query_bias, value_bias, second_gain, second_bias, output_weight, output_bias, third_gain, third_bias, inner_weight, inner_bias, fourth_gain, fourth_bias, down_weight, down_bias):
    weights = tuple((member.astype(jnp.float32) for member in (first_gain, first_bias, joint_weight, query_bias, value_bias, second_gain, second_bias, output_weight, output_bias, third_gain, third_bias, inner_weight, inner_bias, fourth_gain, fourth_bias, down_weight, down_bias)))
    feature_count = inputs.shape[1]
    blocks = inputs.astype(jnp.float32).reshape(N_BATCH, ROWS, feature_count)

    def forward(block_inputs, block_weights):

        def one_device(device_pair):
            return sublayers(device_pair[0], device_pair[1], block_weights)
        return lax.map(jax.checkpoint(one_device), (block_inputs, seq_lengths))
    result_rows, pullback = jax.vjp(forward, blocks, weights)
    input_rows, gradients = pullback(cotangent.astype(jnp.float32).reshape(N_BATCH, ROWS, feature_count))
    return (result_rows.reshape(-1, feature_count).astype(jnp.bfloat16), input_rows.reshape(-1, feature_count).astype(jnp.bfloat16), gradients[0], gradients[1], gradients[2], gradients[3], gradients[4], gradients[5], gradients[6], gradients[7], gradients[8], gradients[9], gradients[10], gradients[11], gradients[12], gradients[13], gradients[14], gradients[15], gradients[16])
```

```python
import functools

import jax
import jax.numpy as jnp
from jax import lax
from jax.experimental import pallas as pl
from jax.experimental.pallas import tpu as pltpu
from jax.sharding import PartitionSpec as P

HEADS = 12
EPSILON = 1e-05
MASKED = -1e9
F32 = jnp.float32
BF16 = jnp.bfloat16
MESH = pl.DeviceIdType.MESH
GROUP = 16
PAIRS = HEADS // 4
UNITS = 12
Y_FIRST = (1, 4, 7, 10)
Y_GATHER = (1, 3, 5, 7, 9, 11)
GELU_C = 0.7978845608028654
GELU_A = 0.044715


def gray(v):
    return v + (v // 2) * (1 - 2 * (v % 2))


def aligned(v, by):
    return pl.multiple_of(v, by)


def normal(values):
    average = jnp.mean(values, axis=-1, keepdims=True)
    centered = values - average
    spread = jnp.mean(centered * centered, axis=-1, keepdims=True)
    scale = lax.rsqrt(spread + EPSILON)
    return centered * scale, scale


def normal_back(vhat, scale, gain, grad):
    scaled = grad * gain
    first = jnp.mean(scaled, axis=-1, keepdims=True)
    second = jnp.mean(scaled * vhat, axis=-1, keepdims=True)
    return scale * (scaled - first - vhat * second)


def dot(left, right):
    return jnp.dot(left, right, preferred_element_type=F32)


def dot_t(left, right):
    return lax.dot_general(left, right, (((1,), (1,)), ((), ())), preferred_element_type=F32)


def t_dot(left, right):
    return lax.dot_general(left, right, (((0,), (0,)), ((), ())), preferred_element_type=F32)


def by8(values):
    rows = values.shape[0]
    return jnp.sum(values.reshape(rows // 8, 8, values.shape[1]), axis=0)


class Copies:
    def __init__(self, send, recv):
        self.send, self.recv, self.count, self.open = send, recv, 0, []

    def remote(self, src, dst, device):
        at = self.count
        self.count += 1
        return pltpu.make_async_remote_copy(
            src_ref=src,
            dst_ref=dst,
            send_sem=self.send.at[at],
            recv_sem=self.recv.at[at],
            device_id=device,
            device_id_type=MESH,
        )

    def go(self, src, dst, device):
        copy = self.remote(src, dst, device)
        copy.start()
        self.open.append(copy)
        return copy

    def drain(self):
        for copy in self.open:
            copy.wait_send()
        self.open = []


def layer_kernel(
    x_in, cot_in, lens, wj_in, wo_in, wi_in, wd_in,
    first_gain, first_bias, query_bias, value_bias, second_gain, second_bias, output_bias,
    third_gain, third_bias, inner_bias, fourth_gain, fourth_bias, down_bias,
    res_out, grad_out, gj_out, go_out, gi_out, gd_out, bv_out,
    wj, wo, wi, wd, feats, cots, ends, normed, q, k, v, vt, kt, bias, pt, mixed_own, mixed,
    sub, fn, handed, tmp, vh, dg, fs, fs_sib, gi_sib, up, gfn, hgr, hg_sib, gmix, do, dqkv,
    gn_sib, result, stat, cols, bv, bv_in, grads, r1, r2, rz, oy,
    lsem, ssem, rsem,
):
    R, HD = x_in.shape
    D = 2 * HD
    H = R // 2
    FF = wi.shape[1]
    T = 256
    NT = FF // T
    x = lax.axis_index("section")
    b = lax.axis_index("batch")
    base = (b // GROUP) * GROUP
    z, y, c = (b // 4) % 4, (b // 2) % 2, b % 2
    p = gray(z)

    def dev(x_, z_, y_, c_):
        return (x_, base + z_ * 4 + y_ * 2 + c_)

    sib = dev(x, z, y, 1 - c)
    xp = dev(1 - x, z, y, c)
    xc = dev(1 - x, z, y, 1 - c)
    yp = dev(x, z, 1 - y, c)
    nxt = dev(x, gray((p + 1) % 4), y, c)
    prv = dev(x, gray((p + 3) % 4), y, c)
    home = c == x
    away = c != x
    own = aligned(c * H, 32)
    other = aligned((1 - c) * H, 32)
    cp = Copies(ssem, rsem)
    local_count = [0]

    def local(src, dst):
        copy = pltpu.make_async_copy(src, dst, lsem.at[local_count[0]])
        local_count[0] += 1
        copy.start()
        return copy

    wj_copies = [local(wj_in.at[:, pl.ds(aligned(t * D + c * HD, 128), HD)], wj.at[t]) for t in range(3)]
    wo_copy = local(wo_in, wo)
    wi_copy = local(wi_in, wi)
    wd_copy = local(wd_in, wd)

    barrier = pltpu.get_barrier_semaphore()
    for peer in (sib, xp, xc, yp, nxt, prv):
        pl.semaphore_signal(barrier, inc=1, device_id=peer, device_id_type=MESH)
    pl.semaphore_wait(barrier, 6)

    NC = 3
    RC = R // NC
    c_native = [cp.remote(src, dst.at[x], sib) for src, dst in ((x_in, feats), (cot_in, cots))]
    c_ends = cp.remote(ends, ends, sib)
    c_cross = [
        cp.remote(x_in.at[pl.ds(i * RC, RC)], feats.at[x, pl.ds(i * RC, RC)], xp) for i in range(NC)
    ]
    c_pass = [
        cp.remote(feats.at[1 - x, pl.ds(i * RC, RC)], feats.at[1 - x, pl.ds(i * RC, RC)], sib)
        for i in range(NC)
    ]
    cot_cross = cp.remote(cot_in, cots.at[x], xp)
    cot_pass = cp.remote(cots.at[1 - x], cots.at[1 - x], sib)
    l_native = [
        pltpu.make_async_copy(src, dst.at[x], lsem.at[12 + i])
        for i, (src, dst) in enumerate(((x_in, feats), (cot_in, cots)))
    ]

    @pl.when(away)
    def _():
        for copy in c_cross:
            copy.start()
        cot_cross.start()

    @pl.when(home)
    def _():
        c_native[0].start()
        l_native[0].start()
        lane = lax.broadcasted_iota(jnp.int32, (1, 8), 1)
        lengths = lens[...].astype(F32)
        for j in range(8):
            end = jnp.sum(jnp.where(lane <= j, lengths, 0.0), axis=1, keepdims=True)
            ends[j : j + 1, :] = jnp.broadcast_to(end, (1, 128))
        c_ends.start()
        l_native[1].start()
        c_native[1].start()
        l_native[0].wait()

    @pl.when(away)
    def _():
        c_native[0].wait_recv()
        c_ends.wait_recv()

    zeros = jnp.zeros((640 - R, HD), BF16)
    for ref in (q, do):
        ref[R:640, :] = zeros

    key_at = lax.broadcasted_iota(jnp.int32, (R, 128), 0).astype(F32)
    key_segment = sum((key_at >= ends[j : j + 1, :]).astype(F32) for j in range(8))
    for j in range(5):
        query_at = (lax.broadcasted_iota(jnp.int32, (1, 128), 1) + j * 128).astype(F32)
        query_segment = sum((query_at >= ends[i : i + 1, :]).astype(F32) for i in range(8))
        allowed = (key_segment == query_segment) & (key_at <= query_at)
        bias[:, j * 128 : (j + 1) * 128] = jnp.where(allowed, 0.0, MASKED).astype(BF16)

    def feature_rows(at, count):
        return jnp.concatenate([feats[0, pl.ds(at, count)], feats[1, pl.ds(at, count)]], 1).astype(F32)

    for copy in wj_copies:
        copy.wait()
    heads_at = aligned(c * HD, 128)
    own_query_bias = query_bias[:, pl.ds(heads_at, HD)]
    own_value_bias = value_bias[:, pl.ds(heads_at, HD)]
    for i in range(NC):

        @pl.when(home)
        def _():
            c_cross[i].wait_recv()
            c_pass[i].start()

        @pl.when(away)
        def _():
            c_pass[i].wait_recv()

        @pl.loop(0, RC // 48)
        def _(step):
            at = aligned(i * RC + step * 48, 16)
            vhat, _ = normal(feature_rows(at, 48))
            normed[pl.ds(at, 48), :] = (vhat * first_gain[...] + first_bias[...]).astype(BF16)

        rows = normed[i * RC : (i + 1) * RC, :]
        at = pl.ds(i * RC, RC)
        q[at, :] = ((dot(rows, wj[0]) + own_query_bias).astype(BF16) * 0.125).astype(BF16)
        k[at, :] = dot(rows, wj[1]).astype(BF16)
        v[at, :] = (dot(rows, wj[2]) + own_value_bias).astype(BF16)
    vt[:, :R] = v[...].T

    first_half = lax.broadcasted_iota(jnp.int32, (128, 128), 1) < 64

    def split_pair(tile):
        zero = jnp.zeros_like(tile)
        return jnp.concatenate([jnp.where(first_half, tile, zero), jnp.where(first_half, zero, tile)], 0)

    blocks = []
    at = 0
    for j in range(5):
        blocks.append((j, min(128 * (j + 1), R), at))
        at += min(128 * (j + 1), R)
    for pr in range(PAIRS):
        lanes = slice(pr * 128, (pr + 1) * 128)
        for j, nk, at in blocks:
            qs = slice(j * 128, (j + 1) * 128)
            block_bias = bias[:nk, qs].astype(F32)
            scores = dot_t(k[:nk, lanes], split_pair(q[qs, lanes]))
            scores = scores + jnp.concatenate([block_bias, block_bias], 1)
            largest = jnp.max(scores, axis=0, keepdims=True)
            shifted = jnp.exp(scores - largest)
            summed = jnp.sum(shifted, axis=0, keepdims=True)
            probs = (shifted * (1.0 / summed)).astype(BF16)
            pt[pr, at : at + nk, :] = probs
            out = dot(vt[lanes, :nk], probs)
            mixed_own[qs, lanes] = jnp.concatenate([out[:64, :128], out[64:, 128:]], 0).T

    c_mixed = cp.go(
        mixed_own.at[pl.ds(other, H)], mixed.at[:, pl.ds(heads_at, HD)], sib
    )
    mixed[:, pl.ds(heads_at, HD)] = mixed_own[pl.ds(own, H), :]
    kt[:, :R] = k[...].T
    wo_copy.wait()
    c_mixed.wait_recv()
    own_live = (lax.broadcasted_iota(jnp.int32, (H, 1), 0) + c * H).astype(F32) < ends[7:8, 0:1]

    @pl.loop(0, H // 48)
    def _(step):
        at = aligned(step * 48, 16)
        vhat, _ = normal(mixed[pl.ds(at, 48), :])
        sub[pl.ds(own + at, 48), :] = (vhat * second_gain[...] + second_bias[...]).astype(BF16)

    branch = dot(sub[pl.ds(own, H), :], wo[...])
    for i in range(6):
        piece = slice(i * 48, (i + 1) * 48)
        handed[piece, :] = (
            feature_rows(own + i * 48, 48) + (branch[piece] + output_bias[...])
        ).astype(BF16)
        vhat, _ = normal(handed[piece, :].astype(F32))
        fn[pl.ds(own + i * 48, 48), :] = (vhat * third_gain[...] + third_bias[...]).astype(BF16)
    c_sub = cp.go(sub.at[pl.ds(own, H)], sub.at[pl.ds(own, H)], sib)
    c_fn = cp.go(fn.at[pl.ds(own, H)], fn.at[pl.ds(own, H)], sib)

    wi_copy.wait()
    stat[0] = jnp.zeros((H, 128), F32)

    @pl.loop(0, NT)
    def _(tile):
        at = pl.ds(aligned(tile * T, T), T)
        inner = dot(fn[pl.ds(own, H), :], wi[:, at])
        for i in range(9):
            piece = slice(i * 32, (i + 1) * 32)
            u = inner[piece] + inner_bias[:, at]
            square = u * u
            t = jnp.tanh(u * (GELU_C + (GELU_C * GELU_A) * square))
            half = 0.5 * u
            act = half + half * t
            tmp[piece, at] = act
            dg[piece, at] = (
                0.5 + 0.5 * t + (half - half * t * t) * (GELU_C + (3 * GELU_C * GELU_A) * square)
            ).astype(BF16)
            stat[0, piece, :] += act[:, :128] + act[:, 128:]

    mean = jnp.sum(stat[0], axis=1, keepdims=True) * (1.0 / FF)
    stat[1] = jnp.broadcast_to(mean, (H, 128))
    stat[0] = jnp.zeros((H, 128), F32)

    @pl.loop(0, NT)
    def _(tile):
        at = pl.ds(aligned(tile * T, T), T)
        for i in range(9):
            piece = slice(i * 32, (i + 1) * 32)
            m = stat[1, piece, :]
            cen = tmp[piece, at] - jnp.concatenate([m, m], 1)
            sq = cen * cen
            stat[0, piece, :] += sq[:, :128] + sq[:, 128:]

    spread = jnp.sum(stat[0], axis=1, keepdims=True) * (1.0 / FF)
    stat[2] = jnp.broadcast_to(lax.rsqrt(spread + EPSILON), (H, 128))

    @pl.loop(0, NT)
    def _(tile):
        at = pl.ds(aligned(tile * T, T), T)
        for i in range(9):
            piece = slice(i * 32, (i + 1) * 32)
            m, s = stat[1, piece, :], stat[2, piece, :]
            vhat = (tmp[piece, at] - jnp.concatenate([m, m], 1)) * jnp.concatenate([s, s], 1)
            vh[piece, at] = vhat.astype(BF16)
            fs[piece, at] = (vhat * fourth_gain[:, at] + fourth_bias[:, at]).astype(BF16)

    c_fs = [
        cp.go(
            fs.at[:, pl.ds(aligned((2 * i + 1 - c) * D, 128), D)],
            fs_sib.at[:, i * D : (i + 1) * D],
            sib,
        )
        for i in range(2)
    ]

    @pl.when(home)
    def _():
        cot_cross.wait_recv()
        cot_pass.start()
        l_native[1].wait()
        cot_pass.wait_send()

    @pl.when(away)
    def _():
        c_native[1].wait_recv()
        cot_pass.wait_recv()

    @pl.loop(0, R // 48)
    def _(step):
        at = aligned(step * 48, 16)
        alive = (lax.broadcasted_iota(jnp.int32, (48, 1), 0) + at).astype(F32) < ends[7:8, 0:1]
        for h in range(2):
            rows = cots[h, pl.ds(at, 48), :].astype(F32)
            cots[h, pl.ds(at, 48), :] = jnp.where(alive, rows, 0.0).astype(BF16)

    up[:, :HD] = cots[0, pl.ds(own, H), :]
    up[:, HD:] = cots[1, pl.ds(own, H), :]

    events = []

    def units(first, count, left_own, left_sib, right):
        for i in range(count):
            for h in range(2):
                rows = jnp.concatenate([left_own(i, h), left_sib(i, h)], 0)
                grads[first + i, h] = t_dot(rows, right(i)).astype(BF16)
            send_unit(first + i)

    copies = {}
    half_rows = HD // 2
    piece_rows = HD // 8

    def y_rows(y_):
        return pl.ds(aligned(y_ * half_rows, 32), half_rows)

    def z_rows(piece, y_=None):
        y_ = y if y_ is None else y_
        return pl.ds(aligned(y_ * half_rows + piece * piece_rows, 16), piece_rows)

    def add(dst, rows, src, src_rows):
        dst[rows, :] = (dst[rows, :].astype(F32) + src[src_rows, :].astype(F32)).astype(BF16)

    def send_unit(u):
        if u in Y_FIRST:
            for h in range(2):
                copies[u, "a", h] = cp.go(
                    grads.at[u, h, y_rows(1 - y)], r1.at[u, h * half_rows : (h + 1) * half_rows], yp
                )
        else:
            copies[u, "a"] = cp.go(grads.at[u, 1 - x], r1.at[u], xp)

    def second(u):
        mine = grads.at[u, x]
        if u in Y_FIRST:
            for h in range(2):
                copies[u, "a", h].wait_recv()
            theirs = grads.at[u, 1 - x]
            add(theirs, y_rows(y), r1.at[u], y_rows(1 - x))
            copies[u, "b"] = cp.go(theirs.at[y_rows(y)], r2.at[u], xp)
            add(mine, y_rows(y), r1.at[u], y_rows(x))
        else:
            copies[u, "a"].wait_recv()
            add(mine, y_rows(1 - y), r1.at[u], y_rows(1 - y))
            copies[u, "b"] = cp.go(mine.at[y_rows(1 - y)], r2.at[u], yp)
            add(mine, y_rows(y), r1.at[u], y_rows(y))

    def third(u):
        mine = grads.at[u, x]
        copies[u, "b"].wait_recv()
        for s in range(4):
            piece = (p + 3 - s) % 4
            add(mine, z_rows(piece), r2.at[u], pl.ds(aligned(piece * piece_rows, 16), piece_rows))
            if s == 0:
                copies[u, "z", 0] = cp.go(mine.at[z_rows(piece)], rz.at[u, 0], nxt)

    def whole(u):
        return oy.at[Y_FIRST.index(u)] if u in Y_FIRST else r1.at[u]

    def ring(u, s):
        mine = grads.at[u, x]
        copies[u, "z", s].wait_recv()
        piece = (p + 2 - s) % 4
        if s < 2:
            add(mine, z_rows(piece), rz.at[u, s], pl.ds(0, piece_rows))
            copies[u, "z", s + 1] = cp.go(mine.at[z_rows(piece)], rz.at[u, s + 1], nxt)
        else:
            out = whole(u)
            out[z_rows(p), :] = (
                mine[z_rows(p), :].astype(F32) + rz[u, 2].astype(F32)
            ).astype(BF16)
            if u in Y_GATHER:
                copies[u, "gy"] = cp.go(out.at[z_rows(p)], out.at[z_rows(p)], yp)
            else:
                copies[u, "gz", 0] = [cp.go(out.at[z_rows(p)], out.at[z_rows(p)], nxt)]

    def gather_z(u, s):
        out = whole(u)
        for copy in copies[u, "gz", s]:
            copy.wait_recv()
        piece = (p + 3 - s) % 4
        sides = (0, 1) if u in Y_GATHER else (y,)
        if s < 2:
            copies[u, "gz", s + 1] = [
                cp.go(out.at[z_rows(piece, side)], out.at[z_rows(piece, side)], nxt)
                for side in sides
            ]
        elif u in Y_GATHER:
            deliver(u)
        else:
            copies[u, "gy"] = cp.go(out.at[y_rows(y)], out.at[y_rows(y)], yp)

    def gather_y(u):
        copies[u, "gy"].wait_recv()
        out = whole(u)
        if u in Y_GATHER:
            copies[u, "gz", 0] = [
                cp.go(out.at[z_rows(p, side)], out.at[z_rows(p, side)], nxt) for side in (0, 1)
            ]
        else:
            deliver(u)

    deliveries = []

    def deliver(u):
        if u < 4:
            target = gd_out.at[pl.ds(aligned(c * D + (u // 2) * HD, 128), HD), (u % 2) * HD : (u % 2 + 1) * HD]
        elif u < 8:
            target = gi_out.at[:, pl.ds(aligned(c * (FF // 2) + (u - 4) * HD, 128), HD)]
        elif u == 8:
            target = go_out.at[:, pl.ds(heads_at, HD)]
        else:
            target = gj_out.at[:, pl.ds(aligned((u - 9) * D + c * HD, 128), HD)]
        copy = cp.go(whole(u), target, sib)
        deliveries.append((copy, local(whole(u), target)))

    def steps_of(u):
        steps = [functools.partial(second, u), functools.partial(third, u)]
        steps += [functools.partial(ring, u, s) for s in range(3)]
        gather = [functools.partial(gather_z, u, s) for s in range(3)]
        if u in Y_GATHER:
            return steps + [functools.partial(gather_y, u)] + gather
        return steps + gather + [functools.partial(gather_y, u)]

    for copy in c_fs:
        copy.wait_recv()
    units(
        0, 4,
        lambda i, h: fs[:, pl.ds(aligned((2 * h + c) * D + (i // 2) * HD, 128), HD)],
        lambda i, h: fs_sib[:, h * D + (i // 2) * HD : h * D + (i // 2 + 1) * HD],
        lambda i: jnp.concatenate([cots[i % 2, pl.ds(own, H), :], cots[i % 2, pl.ds(other, H), :]], 0),
    )

    wd_copy.wait()
    c_result = [
        cp.remote(result.at[0, x], res_out.at[pl.ds(own, H)], sib),
        cp.remote(result.at[0, 1 - x], res_out.at[pl.ds(own, H)], xp),
        cp.remote(result.at[0, 1 - x], res_out.at[pl.ds(own, H)], xc),
        cp.remote(result.at[1, x], grad_out.at[pl.ds(own, H)], sib),
        cp.remote(result.at[1, 1 - x], grad_out.at[pl.ds(own, H)], xp),
        cp.remote(result.at[1, 1 - x], grad_out.at[pl.ds(own, H)], xc),
    ]
    l_result = [
        pltpu.make_async_copy(result.at[i, x], o.at[pl.ds(own, H)], lsem.at[14 + i])
        for i, o in enumerate((res_out, grad_out))
    ]

    def hand_out(i):
        @pl.when(home)
        def _():
            l_result[i].start()
            c_result[3 * i + 1].start()

        @pl.when(away)
        def _():
            c_result[3 * i].start()
            c_result[3 * i + 2].start()

    def handed_out(i):
        @pl.when(home)
        def _():
            l_result[i].wait()
            c_result[3 * i + 1].wait_send()
            c_result[3 * i].wait_recv()

        @pl.when(away)
        def _():
            c_result[3 * i].wait_send()
            c_result[3 * i + 2].wait_send()
            c_result[3 * i + 1].wait_recv()
            c_result[3 * i + 2].wait_recv()

    branch = dot(fs[...], wd[...])
    for i in range(6):
        piece = slice(i * 48, (i + 1) * 48)
        alive = own_live[piece]
        rows = handed[piece, :].astype(F32) + (branch[piece] + down_bias[...])
        rows = jnp.where(alive, rows, 0.0).astype(BF16)
        result[0, 0, piece, :] = rows[:, :HD]
        result[0, 1, piece, :] = rows[:, HD:]
    hand_out(0)

    stat[0] = jnp.zeros((H, 128), F32)
    stat[1] = jnp.zeros((H, 128), F32)

    @pl.loop(0, NT)
    def _(tile):
        at = pl.ds(aligned(tile * T, T), T)
        grad = dot_t(up[...], wd[at, :])
        total_gain = jnp.zeros((8, T), F32)
        total_bias = jnp.zeros((8, T), F32)
        for i in range(9):
            piece = slice(i * 32, (i + 1) * 32)
            g = grad[piece]
            vhat = vh[piece, at].astype(F32)
            tmp[piece, at] = g
            gv = g * vhat
            total_gain += by8(gv)
            total_bias += by8(g)
            gain = fourth_gain[:, at]
            g, gv = g * gain, gv * gain
            stat[0, piece, :] += g[:, :128] + g[:, 128:]
            stat[1, piece, :] += gv[:, :128] + gv[:, 128:]
        cols[0, tile] = total_gain
        cols[1, tile] = total_bias

    for i in range(2):
        mean = jnp.sum(stat[i], axis=1, keepdims=True) * (1.0 / FF)
        stat[i] = jnp.broadcast_to(mean, (H, 128))
    for copy in c_fs:
        copy.wait_send()
    gi = fs

    @pl.loop(0, NT)
    def _(tile):
        at = pl.ds(aligned(tile * T, T), T)
        total = jnp.zeros((8, T), F32)
        for i in range(9):
            piece = slice(i * 32, (i + 1) * 32)
            m1, m2, s = stat[0, piece, :], stat[1, piece, :], stat[2, piece, :]
            vhat = vh[piece, at].astype(F32)
            grad = tmp[piece, at] * fourth_gain[:, at] - jnp.concatenate([m1, m1], 1)
            grad = (grad - vhat * jnp.concatenate([m2, m2], 1)) * jnp.concatenate([s, s], 1)
            low = (grad * dg[piece, at].astype(F32)).astype(BF16)
            gi[piece, at] = low
            total += by8(low.astype(F32))
        cols[2, tile] = total

    c_gi = cp.go(gi.at[:, pl.ds(aligned((1 - c) * (FF // 2), 128), FF // 2)], gi_sib, sib)
    gfn[...] = dot_t(gi[...], wi[...])

    total_gain = jnp.zeros((8, D), F32)
    total_bias = jnp.zeros((8, D), F32)
    total_out = jnp.zeros((8, D), F32)
    for i in range(6):
        piece = slice(i * 48, (i + 1) * 48)
        vhat, scale = normal(handed[piece, :].astype(F32))
        grad = gfn[piece, :]
        total_gain += by8(grad * vhat)
        total_bias += by8(grad)
        low = (
            up[piece, :].astype(F32) + normal_back(vhat, scale, third_gain[...], grad)
        ).astype(BF16)
        hgr[piece, :] = low
        total_out += by8(low.astype(F32))

    def store_vector(row, total):
        bv[row : row + 1, :] = jnp.sum(total, axis=0, keepdims=True)

    store_vector(6, total_out)
    store_vector(7, total_gain)
    store_vector(8, total_bias)
    c_hg = cp.go(hgr.at[:, pl.ds(aligned((1 - c) * HD, 128), HD)], hg_sib, sib)

    gfn[...] = dot_t(hgr[...], wo[...])
    total_gain = jnp.zeros((8, D), F32)
    total_bias = jnp.zeros((8, D), F32)
    for i in range(6):
        piece = slice(i * 48, (i + 1) * 48)
        vhat, scale = normal(mixed[piece, :])
        grad = gfn[piece, :]
        total_gain += by8(grad * vhat)
        total_bias += by8(grad)
        gmix[piece, :] = normal_back(vhat, scale, second_gain[...], grad).astype(BF16)
    store_vector(4, total_gain)
    store_vector(5, total_bias)
    c_gmix = cp.go(
        gmix.at[:, pl.ds(aligned((1 - c) * HD, 128), HD)], do.at[pl.ds(own, H)], sib
    )
    do[pl.ds(own, H), :] = gmix[:, pl.ds(heads_at, HD)]

    c_fn.wait_recv()
    c_gi.wait_recv()

    def fn_rows(at):
        return lambda i, h: fn[pl.ds(at, H), h * HD : (h + 1) * HD]

    units(
        4, 4, fn_rows(own), fn_rows(other),
        lambda i: jnp.concatenate(
            [gi[:, pl.ds(aligned(c * (FF // 2) + i * HD, 128), HD)], gi_sib[:, i * HD : (i + 1) * HD]], 0
        ),
    )
    c_sub.wait_recv()
    c_hg.wait_recv()

    def sub_rows(at):
        return lambda i, h: sub[pl.ds(at, H), h * HD : (h + 1) * HD]

    units(
        8, 1, sub_rows(own), sub_rows(other),
        lambda i: jnp.concatenate([hgr[:, pl.ds(heads_at, HD)], hg_sib[...]], 0),
    )

    c_gmix.wait_recv()
    for pr in range(PAIRS):
        lanes = slice(pr * 128, (pr + 1) * 128)
        for j, nk, at in reversed(blocks):
            qs = slice(j * 128, (j + 1) * 128)
            probs = pt[pr, at : at + nk, :]
            do_split = split_pair(do[qs, lanes])
            grad_probs = dot_t(v[:nk, lanes], do_split)
            exact = probs.astype(F32)
            inner_sum = jnp.sum(exact * grad_probs, axis=0, keepdims=True)
            grad_scores = (exact * (grad_probs - inner_sum)).astype(BF16)
            value_part = dot(probs, do_split)
            key_part = dot(grad_scores, split_pair(q[qs, lanes]))
            if j == len(blocks) - 1:
                gfn[:, :128] = value_part[:H]
                gfn[:, 128:256] = value_part[H:]
                gfn[:, 256:384] = key_part[:H]
                gfn[:, 384:512] = key_part[H:]
            else:
                for lane_at, part in ((0, value_part), (256, key_part)):
                    top = min(nk, H)
                    gfn[:top, lane_at : lane_at + 128] += part[:top]
                    if nk > H:
                        gfn[: nk - H, lane_at + 128 : lane_at + 256] += part[H:]
            out = dot(kt[lanes, :nk], grad_scores)
            query_part = jnp.concatenate([out[:64, :128], out[64:, 128:]], 0).T * 0.125
            count = min(128, R - j * 128)
            dqkv[j * 128 : j * 128 + count, lanes] = query_part[:count].astype(BF16)
        for half in range(2):
            rows = slice(half * H, (half + 1) * H)
            dqkv[rows, 2 * HD + pr * 128 : 2 * HD + (pr + 1) * 128] = gfn[
                :, half * 128 : (half + 1) * 128
            ].astype(BF16)
            dqkv[rows, HD + pr * 128 : HD + (pr + 1) * 128] = gfn[
                :, 256 + half * 128 : 256 + (half + 1) * 128
            ].astype(BF16)

    for i in range(3):
        for h in range(2):
            grads[9 + i, h] = t_dot(
                normed[:, h * HD : (h + 1) * HD], dqkv[:, i * HD : (i + 1) * HD]
            ).astype(BF16)
        send_unit(9 + i)
    bv[2:4, :] = jnp.zeros((2, D), F32)
    for row, at in ((2, 0), (3, 2 * HD)):
        total = jnp.zeros((8, HD), F32)
        for i in range(12):
            total += by8(dqkv[i * 48 : (i + 1) * 48, at : at + HD].astype(F32))
        bv[row : row + 1, pl.ds(heads_at, HD)] = jnp.sum(total, axis=0, keepdims=True)

    for part, at in ((0, other), (1, own)):
        total = jnp.zeros((H, D), F32)
        for i in range(3):
            total += dot_t(dqkv[pl.ds(at, H), i * HD : (i + 1) * HD], wj[i])
        tmp[:, part * D : (part + 1) * D] = total
        if part == 0:
            c_gn = cp.go(tmp.at[:, :D], gn_sib, sib)
    c_gn.wait_recv()
    total_gain = jnp.zeros((8, D), F32)
    total_bias = jnp.zeros((8, D), F32)
    total_down = jnp.zeros((8, D), F32)
    for i in range(6):
        piece = slice(i * 48, (i + 1) * 48)
        vhat, scale = normal(feature_rows(own + i * 48, 48))
        grad = tmp[piece, D : 2 * D] + gn_sib[piece, :]
        total_gain += by8(grad * vhat)
        total_bias += by8(grad)
        total_down += by8(up[piece, :].astype(F32))
        rows = (
            hgr[piece, :].astype(F32) + normal_back(vhat, scale, first_gain[...], grad)
        ).astype(BF16)
        result[1, 0, piece, :] = rows[:, :HD]
        result[1, 1, piece, :] = rows[:, HD:]
    hand_out(1)
    store_vector(0, total_gain)
    store_vector(1, total_bias)
    store_vector(9, total_down)
    for kind, row in ((2, 10), (0, 14), (1, 18)):
        for tile in range(NT):
            bv[row + tile // 3 : row + tile // 3 + 1, (tile % 3) * T : (tile % 3 + 1) * T] = jnp.sum(
                cols[kind, tile], axis=0, keepdims=True
            )
    bv[22:24, :] = jnp.zeros((2, D), F32)

    def vector_step(i):
        if i > 0:
            copies["v", i - 1].wait_recv()
            copies["v", i - 1].wait_send()
            if i <= 3:
                bv[...] += bv_in[i - 1]
            elif i < 6:
                vector_total[0] = vector_total[0] + bv_in[i - 1]
            else:
                bv[...] = vector_total[0] + bv_in[i - 1]
                copies["v", "out"] = local(bv, bv_out)
                return
        if i == 3:
            vector_total.append(bv[...])
        source = bv if i <= 3 else bv_in.at[i - 1]
        copies["v", i] = cp.go(source, bv_in.at[i], (sib, xp, yp, nxt, nxt, nxt)[i])

    vector_total = []
    queues = {u: steps_of(u) for u in range(UNITS)}
    queues["v"] = [functools.partial(vector_step, i) for i in range(7)]
    for tick in range(60):
        for u in range(UNITS):
            if tick >= u and queues[u]:
                queues[u].pop(0)()
        if tick >= 4 and queues["v"]:
            queues["v"].pop(0)()

    @pl.when(home)
    def _():
        for copy in c_native + [c_ends] + c_pass:
            copy.wait_send()

    @pl.when(away)
    def _():
        for copy in c_cross + [cot_cross]:
            copy.wait_send()

    handed_out(0)
    handed_out(1)
    for copy, here in deliveries:
        copy.wait_recv()
        here.wait()
    copies["v", "out"].wait()
    done = [copies["v", i] for i in range(6)] + c_fs
    for copy in cp.open:
        if not any(copy is other for other in done):
            copy.wait_send()


def finish_kernel(gj, go, gi, gd, bv, oj, oo, oi, od, *vectors):
    oj[...] = gj[...].astype(F32)
    oo[...] = go[...].astype(F32)
    oi[...] = gi[...].astype(F32)
    od[...] = gd[...].astype(F32)

    @pl.when(pl.program_id(0) == 0)
    def _():
        x = lax.axis_index("section")
        HD = oo.shape[1] // 2
        at = pl.ds(aligned(x * HD, 128), HD)
        for row in range(10):
            vectors[row][...] = bv[row : row + 1, at]
        for i in range(3):
            row = 10 + 4 * i
            for j in range(2):
                low, high = bv[row + j : row + j + 1, :], bv[row + 2 + j : row + 3 + j, :]
                vectors[10 + i][:, 2 * j * HD : 2 * (j + 1) * HD] = jnp.where(x == 0, low, high)


def per_device(
    inputs, seq_lengths, cotangent,
    first_gain, first_bias, joint_weight, query_bias, value_bias, second_gain, second_bias,
    output_weight, output_bias, third_gain, third_bias, inner_weight, inner_bias,
    fourth_gain, fourth_bias, down_weight, down_bias,
):
    R, HD = inputs.shape
    D, H, FF = 2 * HD, R // 2, inner_weight.shape[1]
    hbm = pl.BlockSpec(memory_space=pl.ANY)
    vmem = pl.BlockSpec(memory_space=pltpu.VMEM)
    flat = [
        m.reshape(1, -1)
        for m in (
            first_gain, first_bias, query_bias, value_bias, second_gain, second_bias, output_bias,
            third_gain, third_bias, inner_bias, fourth_gain, fourth_bias, down_bias,
        )
    ]
    V = pltpu.VMEM
    scratch = [
        V((3, D, HD), BF16), V((D, D), BF16), V((D, FF), BF16), V((FF, D), BF16),
        V((2, R, HD), BF16), V((2, R, HD), BF16), V((8, 128), F32), V((R, D), BF16),
        V((640, HD), BF16), V((R, HD), BF16), V((R, HD), BF16),
        V((HD, 640), BF16), V((HD, 640), BF16), V((R, 640), BF16),
        V((PAIRS, 128 * 10 + R, 256), BF16),
        V((640, HD), F32), V((H, D), F32),
        V((R, D), BF16), V((R, D), BF16), V((H, D), BF16),
        V((H, FF), F32), V((H, FF), BF16), V((H, FF), BF16),
        V((H, FF), BF16), V((H, FF // 2), BF16), V((H, FF // 2), BF16),
        V((H, D), BF16), V((H, D), F32), V((H, D), BF16), V((H, HD), BF16),
        V((H, D), BF16), V((640, HD), BF16), V((R, 3 * HD), BF16),
        V((H, D), F32), V((2, 2, H, HD), BF16), V((3, H, 128), F32),
        V((3, FF // 256, 8, 256), F32), V((24, D), F32), V((6, 24, D), F32),
        V((UNITS, 2, HD, HD), BF16), V((UNITS, HD, HD), BF16), V((UNITS, HD // 2, HD), BF16),
        V((UNITS, 3, HD // 8, HD), BF16), V((len(Y_FIRST), HD, HD), BF16),
        pltpu.SemaphoreType.DMA((32,)), pltpu.SemaphoreType.DMA((200,)), pltpu.SemaphoreType.DMA((200,)),
    ]
    shape = jax.ShapeDtypeStruct
    result, input_grad, gj, go, gi, gd, bv = pl.pallas_call(
        layer_kernel,
        out_shape=[
            shape((R, HD), BF16), shape((R, HD), BF16),
            shape((HD, 3 * D), BF16), shape((HD, D), BF16), shape((HD, FF), BF16),
            shape((FF // 2, D), BF16), shape((24, D), F32),
        ],
        in_specs=[hbm, hbm, vmem, hbm, hbm, hbm, hbm] + [vmem] * 13,
        out_specs=[hbm] * 7,
        scratch_shapes=scratch,
        compiler_params=pltpu.CompilerParams(
            collective_id=0, has_side_effects=True, vmem_limit_bytes=66_000_000
        ),
        cost_estimate=pl.CostEstimate(flops=16 * 10**9, bytes_accessed=25 * 10**6, transcendentals=4 * 10**6),
    )(inputs, cotangent, seq_lengths, joint_weight, output_weight, inner_weight, down_weight, *flat)
    steps = 8
    wide = [(HD, 3 * D), (HD, D), (HD, FF), (FF // 2, D)]

    def block(rows, columns):
        return pl.BlockSpec((rows // steps, columns), lambda i: (i, 0))

    def fixed(rows, columns):
        return pl.BlockSpec((rows, columns), lambda i: (0, 0))

    small = [(1, HD)] * 10 + [(1, FF // 2)] * 3
    groups = lax.axis_size("batch") // GROUP
    if groups > 1:
        peers = [[r + GROUP * g for g in range(groups)] for r in range(GROUP)]
        gj, go, gi, gd, bv = lax.psum(
            tuple(m.astype(F32) for m in (gj, go, gi, gd, bv)), "batch", axis_index_groups=peers
        )
    outs = pl.pallas_call(
        finish_kernel,
        grid=(steps,),
        out_shape=[shape(s, F32) for s in wide + small],
        in_specs=[block(*s) for s in wide] + [fixed(24, D)],
        out_specs=[block(*s) for s in wide] + [fixed(*s) for s in small],
        compiler_params=pltpu.CompilerParams(vmem_limit_bytes=48 * 2**20),
    )(gj, go, gi, gd, bv)
    dj, dout, di, dd = outs[:4]
    vec = [m.reshape(-1) for m in outs[4:]]
    fg, fb, qb, vb, sg, sb, ob, tg, tb, db, ib, hg, hb = vec
    return (
        result, input_grad, fg, fb, dj, qb, vb, sg, sb, dout, ob, tg, tb, di, ib, hg, hb, dd, db,
    )


def solution(mesh):
    wide = P("section", None)
    line = P("section")
    return jax.shard_map(
        per_device,
        mesh=mesh,
        in_specs=(P("batch", "section"), P("batch", None), P("batch", "section")) + (P(),) * 17,
        out_specs=(
            P("batch", "section"), P("batch", "section"), line, line, wide, line, line, line, line,
            wide, line, line, line, wide, line, line, line, wide, line,
        ),
        check_vma=False,
    )
```

```python
import functools

import jax
import jax.numpy as jnp
from jax import lax
from jax.experimental import pallas as pl
from jax.experimental.pallas import tpu as pltpu
from jax.sharding import PartitionSpec as P

HEADS = 12
EPSILON = 1e-05
MASKED = -1e9
F32 = jnp.float32
BF16 = jnp.bfloat16
MESH = pl.DeviceIdType.MESH
GROUP = 16
PAIRS = HEADS // 4
UNITS = 12
AXES = ("x", "y", "a", "b")
SUM_ORDER = ("axyb", "xyab", "yaxb", "aybx", "abxy", "yaxb", "xayb", "xyab", "yxab", "xyab", "yxab", "yxab")
GATHER_ORDER = ("bay", "bay", "bay", "bay", "bya", "bay", "bay", "bay", "bya", "bay", "bya", "bay")
SCHEDULE = (
    (0, ((0, 0),)),
    (1, ((1, 0),)),
    (2, ((2, 0),)),
    (3, ()),
    ("result", ((3, 0),)),
    ("down_back0", ()),
    ("down_back1", ((0, 1), (1, 1))),
    ("down_back2", ((2, 1),)),
    ("inner_back0", ()),
    ("inner_back1", ()),
    ("gfn", ()),
    ("handed", ((1, 2), (3, 1))),
    ("mixed", ()),
    (4, ((4, 0), (0, 2))),
    (5, ((2, 2), (5, 0))),
    (6, ((6, 0),)),
    (7, ((1, 3), (3, 2))),
    (8, ()),
    ("heads0", ((0, 3), (2, 3))),
    ("heads1", ((7, 0), (8, 0))),
    ("heads2", ((4, 1), (5, 1), (6, 1), (1, 4))),
    (9, ((3, 3),)),
    (10, ((0, 4), (10, 0))),
    (11, ((2, 4), (9, 0))),
    ("joint_back", ()),
    ("end", ((8, 1), ("v", 0), (7, 1), (3, 4), ("v", 1), (5, 2), (4, 2), (11, 0), (6, 2), (10, 1), (1, 5), (9, 1), (0, 5), (2, 5), (3, 5), (7, 2), (1, 6), (0, 6), (2, 6), (3, 6), (8, 2), (11, 1), (7, 3), ("v", 2), (6, 3), (5, 3), (8, 3), (4, 3), (7, 4), (9, 2), (6, 4), (10, 2), (5, 4), (1, 7), (9, 3), (8, 4), (11, 2), (7, 5), (10, 3), (0, 7), (6, 5), (5, 5), (2, 7), (11, 3), (9, 4), (7, 6), (8, 5), (3, 7), (10, 4), (6, 6), ("v", 3), (4, 4), (5, 6), (11, 4), (9, 5), (7, 7), (10, 5), ("v", 4), (8, 6), (4, 5), (11, 5), (9, 6), (6, 7), ("v", 5), (5, 7), (8, 7), (10, 6), (11, 6), (4, 6), (9, 7), (10, 7), (11, 7), (4, 7))),
)
GELU_C = 0.7978845608028654
GELU_A = 0.044715


def aligned(v, by):
    return pl.multiple_of(v, by)


def normal(values):
    average = jnp.mean(values, axis=-1, keepdims=True)
    centered = values - average
    spread = jnp.mean(centered * centered, axis=-1, keepdims=True)
    scale = lax.rsqrt(spread + EPSILON)
    return centered * scale, scale


def normal_back(vhat, scale, gain, grad):
    scaled = grad * gain
    first = jnp.mean(scaled, axis=-1, keepdims=True)
    second = jnp.mean(scaled * vhat, axis=-1, keepdims=True)
    return scale * (scaled - first - vhat * second)


def dot(left, right):
    return jnp.dot(left, right, preferred_element_type=F32)


def dot_t(left, right):
    return lax.dot_general(left, right, (((1,), (1,)), ((), ())), preferred_element_type=F32)


def t_dot(left, right):
    return lax.dot_general(left, right, (((0,), (0,)), ((), ())), preferred_element_type=F32)


def by8(values):
    rows = values.shape[0]
    return jnp.sum(values.reshape(rows // 8, 8, values.shape[1]), axis=0)


class Copies:
    def __init__(self, send, recv):
        self.send, self.recv, self.count, self.open = send, recv, 0, []

    def remote(self, src, dst, device):
        at = self.count
        self.count += 1
        return pltpu.make_async_remote_copy(
            src_ref=src,
            dst_ref=dst,
            send_sem=self.send.at[at],
            recv_sem=self.recv.at[at],
            device_id=device,
            device_id_type=MESH,
        )

    def go(self, src, dst, device, keep=True):
        copy = self.remote(src, dst, device)
        copy.start()
        if keep:
            self.open.append(copy)
        return copy

    def drain(self):
        for copy in self.open:
            copy.wait_send()


class Sums:
    def __init__(self, cp, here, peers, grads, parts, whole, bv, bv_in, deliver):
        self.cp, self.here, self.peers, self.deliver = cp, here, peers, deliver
        self.grads, self.parts, self.whole = grads, parts, whole
        self.bv, self.bv_in, self.copies = bv, bv_in, {}

    def send_part(self, u, k):
        order = SUM_ORDER[u]
        fixed = {axis: self.here[axis] for axis in order[:k]}
        fixed[order[k]] = 1 - self.here[order[k]]
        at = (u,) + tuple(fixed.get(axis, slice(None)) for axis in AXES)
        self.copies[u] = self.cp.go(self.grads.at[at], self.parts[k].at[u], self.peers[order[k]])

    def add_part(self, u, k, **side):
        fixed = {axis: self.here[axis] for axis in SUM_ORDER[u][: k + 1]}
        free = [axis for axis in AXES if axis not in fixed]
        at = (u,) + tuple({**side, **fixed}.get(axis, slice(None)) for axis in AXES)
        part = (u,) + tuple(side.get(axis, slice(None)) for axis in free)
        total = self.grads[at].astype(F32) + self.parts[k][part].astype(F32)
        return at, total.astype(BF16)

    def send_gather(self, u, k):
        order = GATHER_ORDER[u]
        at = (u,) + tuple(
            self.here[axis] if axis in order[k:] else slice(None) for axis in AXES[1:]
        )
        self.copies[u] = self.cp.go(self.whole.at[at], self.whole.at[at], self.peers[order[k]])

    def step(self, u, i):
        if u == "v":
            self.vector(i)
            return
        if i > 0:
            self.copies[u].wait_recv()
        if i == 0:
            self.send_part(u, 0)
        elif i < 4:
            axis = SUM_ORDER[u][i]
            at, total = self.add_part(u, i - 1, **{axis: 1 - self.here[axis]})
            self.grads[at] = total
            self.send_part(u, i)
            at, total = self.add_part(u, i - 1, **{axis: self.here[axis]})
            self.grads[at] = total
        elif i == 4:
            at, total = self.add_part(u, 3)
            self.whole[(u,) + at[2:]] = total
            self.send_gather(u, 0)
        elif i < 7:
            self.send_gather(u, i - 4)
        else:
            self.deliver(u, self.whole.at[u])

    def vector(self, i):
        if i > 0:
            self.copies["v"].wait_recv()
            self.copies["v"].wait_send()
            self.bv[...] += self.bv_in[i - 1]
        if i < 5:
            to = self.peers[("c", *AXES)[i]]
            self.copies["v"] = self.cp.go(self.bv, self.bv_in.at[i], to, keep=False)
        else:
            self.deliver("v", self.bv)


def layer_kernel(
    x_in, cot_in, lens, wj_in, wo_in, wi_in, wd_in,
    first_gain, first_bias, query_bias, value_bias, second_gain, second_bias, output_bias,
    third_gain, third_bias, down_bias, inner_bias, fourth_gain, fourth_bias,
    res_out, grad_out, gj_out, go_out, gi_out, gd_out, bv_out,
    wj, wo, wi, wd, feats, cots, ends, normed, q, k, v, vt, kt, bias, pt, mixed_own, mixed,
    sub, fn, handed, tmp, vh, dg, fs, fs_sib, gi_sib, up, gfn, hgr, hg_sib, gmix, do, dqkv,
    result, stat, cols, bv, bv_in, grads, r1, r2, r3, r4, whole,
    vectors, lsem, ssem, rsem,
):
    R, HD = x_in.shape
    D = 2 * HD
    H = R // 2
    FF = wi.shape[1]
    T = 256
    NT = FF // T
    x = lax.axis_index("section")
    b = lax.axis_index("batch")
    base = (b // GROUP) * GROUP
    z, y, c = (b // 4) % 4, (b // 2) % 2, b % 2
    low, high = z % 2, z // 2

    def dev(x_, z_, y_, c_):
        return (x_, base + z_ * 4 + y_ * 2 + c_)

    sib = dev(x, z, y, 1 - c)
    xp = dev(1 - x, z, y, c)
    xc = dev(1 - x, z, y, 1 - c)
    yp = dev(x, z, 1 - y, c)
    peers = {
        "c": sib, "x": xp, "y": yp,
        "a": dev(x, 2 * high + 1 - low, y, c), "b": dev(x, 2 * (1 - high) + low, y, c),
    }
    home = c == x
    away = c != x
    own = aligned(c * H, 32)
    other = aligned((1 - c) * H, 32)
    cp = Copies(ssem, rsem)
    local_count = [0]

    def local(src, dst):
        copy = pltpu.make_async_copy(src, dst, lsem.at[local_count[0]])
        local_count[0] += 1
        copy.start()
        return copy

    wj_copies = [local(wj_in.at[:, pl.ds(aligned(t * D + c * HD, 128), HD)], wj.at[t]) for t in range(3)]
    wo_copy = local(wo_in, wo)
    wi_copy = local(wi_in, wi)
    wd_copy = local(wd_in, wd)

    lines = (
        first_gain, first_bias, query_bias, value_bias, second_gain, second_bias, output_bias,
        third_gain, third_bias, down_bias,
    )
    for i, line in enumerate(lines):
        vectors[i : i + 1, :] = line[...].reshape(1, D)
    (
        first_gain, first_bias, query_bias, value_bias, second_gain, second_bias, output_bias,
        third_gain, third_bias, down_bias,
    ) = (vectors.at[i : i + 1] for i in range(len(lines)))

    barrier = pltpu.get_barrier_semaphore()
    for peer in (*peers.values(), xc):
        pl.semaphore_signal(barrier, inc=1, device_id=peer, device_id_type=MESH)
    pl.semaphore_wait(barrier, 6)

    NC = 3
    RC = R // NC
    c_native = [cp.remote(src, dst.at[x], sib) for src, dst in ((x_in, feats), (cot_in, cots))]
    c_ends = cp.remote(ends, ends, sib)
    c_cross = [
        cp.remote(x_in.at[pl.ds(i * RC, RC)], feats.at[x, pl.ds(i * RC, RC)], xp) for i in range(NC)
    ]
    c_pass = [
        cp.remote(feats.at[1 - x, pl.ds(i * RC, RC)], feats.at[1 - x, pl.ds(i * RC, RC)], sib)
        for i in range(NC)
    ]
    cot_cross = cp.remote(cot_in, cots.at[x], xp)
    cot_pass = cp.remote(cots.at[1 - x], cots.at[1 - x], sib)
    l_native = [
        pltpu.make_async_copy(src, dst.at[x], lsem.at[12 + i])
        for i, (src, dst) in enumerate(((x_in, feats), (cot_in, cots)))
    ]

    @pl.when(away)
    def _():
        for copy in c_cross:
            copy.start()
        cot_cross.start()

    @pl.when(home)
    def _():
        c_native[0].start()
        l_native[0].start()
        lane = lax.broadcasted_iota(jnp.int32, (1, 8), 1)
        lengths = lens[...].astype(F32)
        for j in range(8):
            end = jnp.sum(jnp.where(lane <= j, lengths, 0.0), axis=1, keepdims=True)
            ends[j : j + 1, :] = jnp.broadcast_to(end, (1, 128))
        c_ends.start()
        l_native[1].start()
        c_native[1].start()
        l_native[0].wait()

    @pl.when(away)
    def _():
        c_native[0].wait_recv()
        c_ends.wait_recv()

    zeros = jnp.zeros((640 - R, HD), BF16)
    for ref in (q, do):
        ref[R:640, :] = zeros

    key_at = lax.broadcasted_iota(jnp.int32, (R, 128), 0).astype(F32)
    key_segment = sum((key_at >= ends[j : j + 1, :]).astype(F32) for j in range(8))
    for j in range(5):
        query_at = (lax.broadcasted_iota(jnp.int32, (1, 128), 1) + j * 128).astype(F32)
        query_segment = sum((query_at >= ends[i : i + 1, :]).astype(F32) for i in range(8))
        allowed = (key_segment == query_segment) & (key_at <= query_at)
        bias[:, j * 128 : (j + 1) * 128] = jnp.where(allowed, 0.0, MASKED).astype(BF16)

    def feature_rows(at, count):
        return jnp.concatenate([feats[0, pl.ds(at, count)], feats[1, pl.ds(at, count)]], 1).astype(F32)

    for copy in wj_copies:
        copy.wait()
    heads_at = aligned(c * HD, 128)
    own_query_bias = query_bias[:, pl.ds(heads_at, HD)]
    own_value_bias = value_bias[:, pl.ds(heads_at, HD)]
    for i in range(NC):

        @pl.when(home)
        def _():
            c_cross[i].wait_recv()
            c_pass[i].start()

        @pl.when(away)
        def _():
            c_pass[i].wait_recv()

        @pl.loop(0, RC // 48)
        def _(step):
            at = aligned(i * RC + step * 48, 16)
            vhat, _ = normal(feature_rows(at, 48))
            normed[pl.ds(at, 48), :] = (vhat * first_gain[...] + first_bias[...]).astype(BF16)

        rows = normed[i * RC : (i + 1) * RC, :]
        at = pl.ds(i * RC, RC)
        q[at, :] = ((dot(rows, wj[0]) + own_query_bias).astype(BF16) * 0.125).astype(BF16)
        k[at, :] = dot(rows, wj[1]).astype(BF16)
        v[at, :] = (dot(rows, wj[2]) + own_value_bias).astype(BF16)
    vt[:, :R] = v[...].T

    first_half = lax.broadcasted_iota(jnp.int32, (128, 128), 1) < 64

    def split_pair(tile):
        zero = jnp.zeros_like(tile)
        return jnp.concatenate([jnp.where(first_half, tile, zero), jnp.where(first_half, zero, tile)], 0)

    blocks = []
    at = 0
    for j in range(5):
        blocks.append((j, min(128 * (j + 1), R), at))
        at += min(128 * (j + 1), R)
    for pr in range(PAIRS):
        lanes = slice(pr * 128, (pr + 1) * 128)
        for j, nk, at in blocks:
            qs = slice(j * 128, (j + 1) * 128)
            block_bias = bias[:nk, qs].astype(F32)
            scores = dot_t(k[:nk, lanes], split_pair(q[qs, lanes]))
            scores = scores + jnp.concatenate([block_bias, block_bias], 1)
            largest = jnp.max(scores, axis=0, keepdims=True)
            shifted = jnp.exp(scores - largest)
            summed = jnp.sum(shifted, axis=0, keepdims=True)
            probs = (shifted * (1.0 / summed)).astype(BF16)
            pt[pr, at : at + nk, :] = probs
            out = dot(vt[lanes, :nk], probs)
            mixed_own[qs, lanes] = jnp.concatenate([out[:64, :128], out[64:, 128:]], 0).T

    c_mixed = cp.go(
        mixed_own.at[pl.ds(other, H)], mixed.at[:, pl.ds(heads_at, HD)], sib
    )
    mixed[:, pl.ds(heads_at, HD)] = mixed_own[pl.ds(own, H), :]
    kt[:, :R] = k[...].T
    wo_copy.wait()
    c_mixed.wait_recv()
    own_live = (lax.broadcasted_iota(jnp.int32, (H, 1), 0) + c * H).astype(F32) < ends[7:8, 0:1]

    @pl.loop(0, H // 48)
    def _(step):
        at = aligned(step * 48, 16)
        vhat, _ = normal(mixed[pl.ds(at, 48), :])
        sub[pl.ds(own + at, 48), :] = (vhat * second_gain[...] + second_bias[...]).astype(BF16)

    branch = dot(sub[pl.ds(own, H), :], wo[...])
    for i in range(6):
        piece = slice(i * 48, (i + 1) * 48)
        handed[piece, :] = (
            feature_rows(own + i * 48, 48) + (branch[piece] + output_bias[...])
        ).astype(BF16)
        vhat, _ = normal(handed[piece, :].astype(F32))
        fn[pl.ds(own + i * 48, 48), :] = (vhat * third_gain[...] + third_bias[...]).astype(BF16)
    c_sub = cp.go(sub.at[pl.ds(own, H)], sub.at[pl.ds(own, H)], sib)
    c_fn = cp.go(fn.at[pl.ds(own, H)], fn.at[pl.ds(own, H)], sib)

    wi_copy.wait()
    stat[0] = jnp.zeros((H, 128), F32)

    @pl.loop(0, NT)
    def _(tile):
        at = pl.ds(aligned(tile * T, T), T)
        inner = dot(fn[pl.ds(own, H), :], wi[:, at])
        for i in range(9):
            piece = slice(i * 32, (i + 1) * 32)
            u = inner[piece] + inner_bias[:, at]
            square = u * u
            t = jnp.tanh(u * (GELU_C + (GELU_C * GELU_A) * square))
            half = 0.5 * u
            act = half + half * t
            tmp[piece, at] = act
            dg[piece, at] = (
                0.5 + 0.5 * t + (half - half * t * t) * (GELU_C + (3 * GELU_C * GELU_A) * square)
            ).astype(BF16)
            stat[0, piece, :] += act[:, :128] + act[:, 128:]

    mean = jnp.sum(stat[0], axis=1, keepdims=True) * (1.0 / FF)
    stat[1] = jnp.broadcast_to(mean, (H, 128))
    stat[0] = jnp.zeros((H, 128), F32)

    @pl.loop(0, NT)
    def _(tile):
        at = pl.ds(aligned(tile * T, T), T)
        for i in range(9):
            piece = slice(i * 32, (i + 1) * 32)
            m = stat[1, piece, :]
            cen = tmp[piece, at] - jnp.concatenate([m, m], 1)
            sq = cen * cen
            stat[0, piece, :] += sq[:, :128] + sq[:, 128:]

    spread = jnp.sum(stat[0], axis=1, keepdims=True) * (1.0 / FF)
    stat[2] = jnp.broadcast_to(lax.rsqrt(spread + EPSILON), (H, 128))

    @pl.loop(0, NT)
    def _(tile):
        at = pl.ds(aligned(tile * T, T), T)
        for i in range(9):
            piece = slice(i * 32, (i + 1) * 32)
            m, s = stat[1, piece, :], stat[2, piece, :]
            vhat = (tmp[piece, at] - jnp.concatenate([m, m], 1)) * jnp.concatenate([s, s], 1)
            vh[piece, at] = vhat.astype(BF16)
            fs[piece, at] = (vhat * fourth_gain[:, at] + fourth_bias[:, at]).astype(BF16)

    c_fs = [
        cp.go(
            fs.at[:, pl.ds(aligned((2 * i + 1 - c) * D, 128), D)],
            fs_sib.at[:, i * D : (i + 1) * D],
            sib,
            keep=False,
        )
        for i in range(2)
    ]

    @pl.when(home)
    def _():
        cot_cross.wait_recv()
        cot_pass.start()
        l_native[1].wait()
        cot_pass.wait_send()

    @pl.when(away)
    def _():
        c_native[1].wait_recv()
        cot_pass.wait_recv()

    @pl.loop(0, R // 48)
    def _(step):
        at = aligned(step * 48, 16)
        alive = (lax.broadcasted_iota(jnp.int32, (48, 1), 0) + at).astype(F32) < ends[7:8, 0:1]
        for h in range(2):
            rows = cots[h, pl.ds(at, 48), :].astype(F32)
            cots[h, pl.ds(at, 48), :] = jnp.where(alive, rows, 0.0).astype(BF16)

    up[:, :HD] = cots[0, pl.ds(own, H), :]
    up[:, HD:] = cots[1, pl.ds(own, H), :]

    deliveries = []

    def deliver(u, total):
        if u == "v":
            deliveries.append((None, local(total, bv_out)))
            return
        rows = (slice(None),) * 4
        if u < 4:
            target = gd_out.at[(c, u // 2) + rows + (slice((u % 2) * HD, (u % 2 + 1) * HD),)]
        elif u < 8:
            target = gi_out.at[rows + (pl.ds(aligned(c * (FF // 2) + (u - 4) * HD, 128), HD),)]
        elif u == 8:
            target = go_out.at[rows + (pl.ds(heads_at, HD),)]
        else:
            target = gj_out.at[rows + (pl.ds(aligned((u - 9) * D + c * HD, 128), HD),)]
        deliveries.append((cp.go(total, target, sib), local(total, target)))

    here = {"x": x, "y": y, "a": low, "b": high}
    sums = Sums(cp, here, peers, grads, (r1, r2, r3, r4), whole, bv, bv_in, deliver)
    schedule = iter(SCHEDULE)

    def pump(mark):
        at, steps = next(schedule)
        assert at == mark
        for u, i in steps:
            sums.step(u, i)


    def cut_rows(unit):
        return unit.astype(BF16).reshape(2, 2, 2, HD // 8, HD)

    def units(first, count, left_own, left_sib, right):
        for i in range(count):
            for h in range(2):
                rows = jnp.concatenate([left_own(i, h), left_sib(i, h)], 0)
                grads[first + i, h] = cut_rows(t_dot(rows, right(i)))
            pump(first + i)

    for copy in c_fs:
        copy.wait_recv()
    units(
        0, 4,
        lambda i, h: fs[:, pl.ds(aligned((2 * h + c) * D + (i // 2) * HD, 128), HD)],
        lambda i, h: fs_sib[:, h * D + (i // 2) * HD : h * D + (i // 2 + 1) * HD],
        lambda i: jnp.concatenate([cots[i % 2, pl.ds(own, H), :], cots[i % 2, pl.ds(other, H), :]], 0),
    )

    wd_copy.wait()
    c_result = [
        cp.remote(result.at[0, x], res_out.at[pl.ds(own, H)], sib),
        cp.remote(result.at[0, 1 - x], res_out.at[pl.ds(own, H)], xp),
        cp.remote(result.at[0, 1 - x], res_out.at[pl.ds(own, H)], xc),
        cp.remote(result.at[1, x], grad_out.at[pl.ds(own, H)], sib),
        cp.remote(result.at[1, 1 - x], grad_out.at[pl.ds(own, H)], xp),
        cp.remote(result.at[1, 1 - x], grad_out.at[pl.ds(own, H)], xc),
    ]
    l_result = [
        pltpu.make_async_copy(result.at[i, x], o.at[pl.ds(own, H)], lsem.at[14 + i])
        for i, o in enumerate((res_out, grad_out))
    ]

    def hand_out(i):
        @pl.when(home)
        def _():
            l_result[i].start()
            c_result[3 * i + 1].start()

        @pl.when(away)
        def _():
            c_result[3 * i].start()
            c_result[3 * i + 2].start()

    def handed_out(i):
        @pl.when(home)
        def _():
            l_result[i].wait()
            c_result[3 * i + 1].wait_send()
            c_result[3 * i].wait_recv()

        @pl.when(away)
        def _():
            c_result[3 * i].wait_send()
            c_result[3 * i + 2].wait_send()
            c_result[3 * i + 1].wait_recv()
            c_result[3 * i + 2].wait_recv()

    branch = dot(fs[...], wd[...])
    for i in range(6):
        piece = slice(i * 48, (i + 1) * 48)
        alive = own_live[piece]
        rows = handed[piece, :].astype(F32) + (branch[piece] + down_bias[...])
        rows = jnp.where(alive, rows, 0.0).astype(BF16)
        result[0, 0, piece, :] = rows[:, :HD]
        result[0, 1, piece, :] = rows[:, HD:]
    hand_out(0)
    pump("result")

    stat[0] = jnp.zeros((H, 128), F32)
    stat[1] = jnp.zeros((H, 128), F32)

    def down_back(tile):
        at = pl.ds(aligned(tile * T, T), T)
        grad = dot_t(up[...], wd[at, :])
        total_gain = jnp.zeros((8, T), F32)
        total_bias = jnp.zeros((8, T), F32)
        for i in range(9):
            piece = slice(i * 32, (i + 1) * 32)
            g = grad[piece]
            vhat = vh[piece, at].astype(F32)
            tmp[piece, at] = g
            gv = g * vhat
            total_gain += by8(gv)
            total_bias += by8(g)
            gain = fourth_gain[:, at]
            g, gv = g * gain, gv * gain
            stat[0, piece, :] += g[:, :128] + g[:, 128:]
            stat[1, piece, :] += gv[:, :128] + gv[:, 128:]
        cols[0, tile] = total_gain
        cols[1, tile] = total_bias

    for i in range(3):
        pl.loop(i * NT // 3, (i + 1) * NT // 3)(down_back)
        pump(f"down_back{i}")

    for i in range(2):
        mean = jnp.sum(stat[i], axis=1, keepdims=True) * (1.0 / FF)
        stat[i] = jnp.broadcast_to(mean, (H, 128))
    for copy in c_fs:
        copy.wait_send()
    gi = fs

    def inner_back(tile):
        at = pl.ds(aligned(tile * T, T), T)
        total = jnp.zeros((8, T), F32)
        for i in range(9):
            piece = slice(i * 32, (i + 1) * 32)
            m1, m2, s = stat[0, piece, :], stat[1, piece, :], stat[2, piece, :]
            vhat = vh[piece, at].astype(F32)
            grad = tmp[piece, at] * fourth_gain[:, at] - jnp.concatenate([m1, m1], 1)
            grad = (grad - vhat * jnp.concatenate([m2, m2], 1)) * jnp.concatenate([s, s], 1)
            low = (grad * dg[piece, at].astype(F32)).astype(BF16)
            gi[piece, at] = low
            total += by8(low.astype(F32))
        cols[2, tile] = total

    for i in range(2):
        pl.loop(i * NT // 2, (i + 1) * NT // 2)(inner_back)
        pump(f"inner_back{i}")

    c_gi = cp.go(gi.at[:, pl.ds(aligned((1 - c) * (FF // 2), 128), FF // 2)], gi_sib, sib)
    gfn[...] = dot_t(gi[...], wi[...])
    pump("gfn")

    total_gain = jnp.zeros((8, D), F32)
    total_bias = jnp.zeros((8, D), F32)
    total_out = jnp.zeros((8, D), F32)
    for i in range(6):
        piece = slice(i * 48, (i + 1) * 48)
        vhat, scale = normal(handed[piece, :].astype(F32))
        grad = gfn[piece, :]
        total_gain += by8(grad * vhat)
        total_bias += by8(grad)
        low = (
            up[piece, :].astype(F32) + normal_back(vhat, scale, third_gain[...], grad)
        ).astype(BF16)
        hgr[piece, :] = low
        total_out += by8(low.astype(F32))

    def store_vector(row, total):
        bv[row : row + 1, :] = jnp.sum(total, axis=0, keepdims=True)

    store_vector(6, total_out)
    store_vector(7, total_gain)
    store_vector(8, total_bias)
    c_hg = cp.go(hgr.at[:, pl.ds(aligned((1 - c) * HD, 128), HD)], hg_sib, sib)

    pump("handed")

    gfn[...] = dot_t(hgr[...], wo[...])
    total_gain = jnp.zeros((8, D), F32)
    total_bias = jnp.zeros((8, D), F32)
    for i in range(6):
        piece = slice(i * 48, (i + 1) * 48)
        vhat, scale = normal(mixed[piece, :])
        grad = gfn[piece, :]
        total_gain += by8(grad * vhat)
        total_bias += by8(grad)
        gmix[piece, :] = normal_back(vhat, scale, second_gain[...], grad).astype(BF16)
    store_vector(4, total_gain)
    store_vector(5, total_bias)
    c_gmix = cp.go(
        gmix.at[:, pl.ds(aligned((1 - c) * HD, 128), HD)], do.at[pl.ds(own, H)], sib
    )
    do[pl.ds(own, H), :] = gmix[:, pl.ds(heads_at, HD)]

    pump("mixed")

    c_fn.wait_recv()
    c_gi.wait_recv()

    def fn_rows(at):
        return lambda i, h: fn[pl.ds(at, H), h * HD : (h + 1) * HD]

    units(
        4, 4, fn_rows(own), fn_rows(other),
        lambda i: jnp.concatenate(
            [gi[:, pl.ds(aligned(c * (FF // 2) + i * HD, 128), HD)], gi_sib[:, i * HD : (i + 1) * HD]], 0
        ),
    )
    c_sub.wait_recv()
    c_hg.wait_recv()

    def sub_rows(at):
        return lambda i, h: sub[pl.ds(at, H), h * HD : (h + 1) * HD]

    units(
        8, 1, sub_rows(own), sub_rows(other),
        lambda i: jnp.concatenate([hgr[:, pl.ds(heads_at, HD)], hg_sib[...]], 0),
    )

    c_gmix.wait_recv()
    for pr in range(PAIRS):
        lanes = slice(pr * 128, (pr + 1) * 128)
        for j, nk, at in reversed(blocks):
            qs = slice(j * 128, (j + 1) * 128)
            probs = pt[pr, at : at + nk, :]
            do_split = split_pair(do[qs, lanes])
            grad_probs = dot_t(v[:nk, lanes], do_split)
            exact = probs.astype(F32)
            inner_sum = jnp.sum(exact * grad_probs, axis=0, keepdims=True)
            grad_scores = (exact * (grad_probs - inner_sum)).astype(BF16)
            value_part = dot(probs, do_split)
            key_part = dot(grad_scores, split_pair(q[qs, lanes]))
            if j == len(blocks) - 1:
                gfn[:, :128] = value_part[:H]
                gfn[:, 128:256] = value_part[H:]
                gfn[:, 256:384] = key_part[:H]
                gfn[:, 384:512] = key_part[H:]
            else:
                for lane_at, part in ((0, value_part), (256, key_part)):
                    top = min(nk, H)
                    gfn[:top, lane_at : lane_at + 128] += part[:top]
                    if nk > H:
                        gfn[: nk - H, lane_at + 128 : lane_at + 256] += part[H:]
            out = dot(kt[lanes, :nk], grad_scores)
            query_part = jnp.concatenate([out[:64, :128], out[64:, 128:]], 0).T * 0.125
            count = min(128, R - j * 128)
            dqkv[j * 128 : j * 128 + count, lanes] = query_part[:count].astype(BF16)
        for half in range(2):
            rows = slice(half * H, (half + 1) * H)
            dqkv[rows, 2 * HD + pr * 128 : 2 * HD + (pr + 1) * 128] = gfn[
                :, half * 128 : (half + 1) * 128
            ].astype(BF16)
            dqkv[rows, HD + pr * 128 : HD + (pr + 1) * 128] = gfn[
                :, 256 + half * 128 : 256 + (half + 1) * 128
            ].astype(BF16)
        pump(f"heads{pr}")

    for i in range(3):
        for h in range(2):
            grads[9 + i, h] = cut_rows(
                t_dot(normed[:, h * HD : (h + 1) * HD], dqkv[:, i * HD : (i + 1) * HD])
            )
        pump(9 + i)
    bv[2:4, :] = jnp.zeros((2, D), F32)
    for row, at in ((2, 0), (3, 2 * HD)):
        total = jnp.zeros((8, HD), F32)
        for i in range(12):
            total += by8(dqkv[i * 48 : (i + 1) * 48, at : at + HD].astype(F32))
        bv[row : row + 1, pl.ds(heads_at, HD)] = jnp.sum(total, axis=0, keepdims=True)

    for part, at in ((0, other), (1, own)):
        total = jnp.zeros((H, D), F32)
        for i in range(3):
            total += dot_t(dqkv[pl.ds(at, H), i * HD : (i + 1) * HD], wj[i])
        tmp[:, part * D : (part + 1) * D] = total
        if part == 0:
            c_gn = cp.go(tmp.at[:, :D], mixed, sib)
    c_gn.wait_recv()
    pump("joint_back")
    total_gain = jnp.zeros((8, D), F32)
    total_bias = jnp.zeros((8, D), F32)
    total_down = jnp.zeros((8, D), F32)
    for i in range(6):
        piece = slice(i * 48, (i + 1) * 48)
        vhat, scale = normal(feature_rows(own + i * 48, 48))
        grad = tmp[piece, D : 2 * D] + mixed[piece, :]
        total_gain += by8(grad * vhat)
        total_bias += by8(grad)
        total_down += by8(up[piece, :].astype(F32))
        rows = (
            hgr[piece, :].astype(F32) + normal_back(vhat, scale, first_gain[...], grad)
        ).astype(BF16)
        result[1, 0, piece, :] = rows[:, :HD]
        result[1, 1, piece, :] = rows[:, HD:]
    hand_out(1)
    store_vector(0, total_gain)
    store_vector(1, total_bias)
    store_vector(9, total_down)
    for kind, row in ((2, 10), (0, 14), (1, 18)):
        for tile in range(NT):
            bv[row + tile // 3 : row + tile // 3 + 1, (tile % 3) * T : (tile % 3 + 1) * T] = jnp.sum(
                cols[kind, tile], axis=0, keepdims=True
            )
    bv[22:24, :] = jnp.zeros((2, D), F32)

    pump("end")

    @pl.when(home)
    def _():
        for copy in c_native + [c_ends] + c_pass:
            copy.wait_send()

    @pl.when(away)
    def _():
        for copy in c_cross + [cot_cross]:
            copy.wait_send()

    handed_out(0)
    handed_out(1)
    for copy, here in deliveries:
        if copy is not None:
            copy.wait_recv()
        here.wait()
    cp.drain()


def finish_kernel(gj, go, gi, gd, bv, res, grad, oj, oo, oi, od, *rest):
    *vectors, res_out, grad_out, sem = rest
    copies = [pltpu.make_async_copy(res, res_out, sem.at[0]), pltpu.make_async_copy(grad, grad_out, sem.at[1])]

    @pl.when(pl.program_id(0) == 0)
    def _():
        for copy in copies:
            copy.start()
        x = lax.axis_index("section")
        HD = oo.shape[1] // 2
        at = pl.ds(aligned(x * HD, 128), HD)
        for row in range(10):
            vectors[row][...] = bv[row : row + 1, at].reshape(HD)
        for i in range(3):
            row = 10 + 4 * i
            halves = [jnp.concatenate([bv[j : j + 1, :], bv[j + 1 : j + 2, :]], 1) for j in (row, row + 2)]
            vectors[10 + i][...] = jnp.where(x == 0, *halves).reshape(4 * HD)

    oj[...] = gj[...].astype(F32)
    oo[...] = go[...].astype(F32)
    oi[...] = gi[...].astype(F32)
    od[...] = gd[...].astype(F32)

    @pl.when(pl.program_id(0) == pl.num_programs(0) - 1)
    def _():
        for copy in copies:
            copy.wait()


def per_device(
    inputs, seq_lengths, cotangent,
    first_gain, first_bias, joint_weight, query_bias, value_bias, second_gain, second_bias,
    output_weight, output_bias, third_gain, third_bias, inner_weight, inner_bias,
    fourth_gain, fourth_bias, down_weight, down_bias,
):
    R, HD = inputs.shape
    D, H, FF = 2 * HD, R // 2, inner_weight.shape[1]
    hbm = pl.BlockSpec(memory_space=pl.ANY)
    vmem = pl.BlockSpec(memory_space=pltpu.VMEM)
    lines = (
        first_gain, first_bias, query_bias, value_bias, second_gain, second_bias, output_bias,
        third_gain, third_bias, down_bias,
    )
    lines += tuple(m.reshape(1, -1) for m in (inner_bias, fourth_gain, fourth_bias))
    V = pltpu.VMEM
    scratch = [
        V((3, D, HD), BF16), V((D, D), BF16), V((D, FF), BF16), V((FF, D), BF16),
        V((2, R, HD), BF16), V((2, R, HD), BF16), V((8, 128), F32), V((R, D), BF16),
        V((640, HD), BF16), V((R, HD), BF16), V((R, HD), BF16),
        V((HD, 640), BF16), V((HD, 640), BF16), V((R, 640), BF16),
        V((PAIRS, 128 * 10 + R, 256), BF16),
        V((640, HD), F32), V((H, D), F32),
        V((R, D), BF16), V((R, D), BF16), V((H, D), BF16),
        V((H, FF), F32), V((H, FF), BF16), V((H, FF), BF16),
        V((H, FF), BF16), V((H, FF // 2), BF16), V((H, FF // 2), BF16),
        V((H, D), BF16), V((H, D), F32), V((H, D), BF16), V((H, HD), BF16),
        V((H, D), BF16), V((640, HD), BF16), V((R, 3 * HD), BF16),
        V((2, 2, H, HD), BF16), V((3, H, 128), F32),
        V((3, FF // 256, 8, 256), F32), V((24, D), F32), V((5, 24, D), F32),
        V((UNITS, 2, 2, 2, 2, HD // 8, HD), BF16),
        V((UNITS, 2, 2, 2, HD // 8, HD), BF16), V((UNITS, 2, 2, HD // 8, HD), BF16),
        V((UNITS, 2, HD // 8, HD), BF16), V((UNITS, HD // 8, HD), BF16),
        V((UNITS, 2, 2, 2, HD // 8, HD), BF16),
        V((10, D), F32), pltpu.SemaphoreType.DMA((32,)), pltpu.SemaphoreType.DMA((200,)), pltpu.SemaphoreType.DMA((200,)),
    ]
    shape = jax.ShapeDtypeStruct
    result, input_grad, gj, go, gi, gd, bv = pl.pallas_call(
        layer_kernel,
        out_shape=[
            shape((R, HD), BF16), shape((R, HD), BF16),
            *(shape((2, 2, 2, HD // 8, n), BF16) for n in (3 * D, D, FF)),
            shape((2, 2, 2, 2, 2, HD // 8, D), BF16), shape((24, D), F32),
        ],
        in_specs=[hbm, hbm, vmem, hbm, hbm, hbm, hbm] + [vmem] * 13,
        out_specs=[hbm] * 7,
        scratch_shapes=scratch,
        compiler_params=pltpu.CompilerParams(
            collective_id=0, has_side_effects=True, vmem_limit_bytes=66_000_000
        ),
        cost_estimate=pl.CostEstimate(flops=16 * 10**9, bytes_accessed=25 * 10**6, transcendentals=4 * 10**6),
    )(inputs, cotangent, seq_lengths, joint_weight, output_weight, inner_weight, down_weight, *lines)
    steps = 8
    wide = [(HD, 3 * D), (HD, D), (HD, FF), (FF // 2, D)]
    gj, go, gi, gd = (m.reshape(s) for m, s in zip((gj, go, gi, gd), wide))

    def block(rows, columns):
        return pl.BlockSpec((rows // steps, columns), lambda i: (i, 0))

    small = [(HD,)] * 10 + [(FF // 2,)] * 3
    groups = lax.axis_size("batch") // GROUP
    if groups > 1:
        peers = [[r + GROUP * g for g in range(groups)] for r in range(GROUP)]
        gj, go, gi, gd, bv = lax.psum(
            tuple(m.astype(F32) for m in (gj, go, gi, gd, bv)), "batch", axis_index_groups=peers
        )
    outs = pl.pallas_call(
        finish_kernel,
        grid=(steps,),
        out_shape=[shape(s, F32) for s in wide + small] + [shape((R, HD), BF16)] * 2,
        in_specs=[block(*s) for s in wide] + [pl.BlockSpec((24, D), lambda i: (0, 0)), hbm, hbm],
        out_specs=[block(*s) for s in wide] + [pl.BlockSpec(s, lambda i: (0,)) for s in small] + [hbm, hbm],
        scratch_shapes=[pltpu.SemaphoreType.DMA((2,))],
        compiler_params=pltpu.CompilerParams(vmem_limit_bytes=66_000_000),
    )(gj, go, gi, gd, bv, result, input_grad)
    result, input_grad = outs[-2:]
    dj, dout, di, dd = outs[:4]
    fg, fb, qb, vb, sg, sb, ob, tg, tb, db, ib, hg, hb = outs[4:-2]
    return (
        result, input_grad, fg, fb, dj, qb, vb, sg, sb, dout, ob, tg, tb, di, ib, hg, hb, dd, db,
    )


def solution(mesh):
    wide = P("section", None)
    line = P("section")
    return jax.shard_map(
        per_device,
        mesh=mesh,
        in_specs=(P("batch", "section"), P("batch", None), P("batch", "section")) + (P(),) * 17,
        out_specs=(
            P("batch", "section"), P("batch", "section"), line, line, wide, line, line, line, line,
            wide, line, line, line, wide, line, line, line, wide, line,
        ),
        check_vma=False,
    )
```

```python
import functools

import jax
import jax.numpy as jnp
from jax import lax
from jax.experimental import pallas as pl
from jax.experimental.pallas import tpu as pltpu
from jax.sharding import PartitionSpec as P

HEADS = 12
EPSILON = 1e-05
MASKED = -1e9
F32 = jnp.float32
BF16 = jnp.bfloat16
MESH = pl.DeviceIdType.MESH
GROUP = 16
PAIRS = HEADS // 4
UNITS = 12
AXES = ("x", "y", "a", "b")
SUM_ORDER = ("yaxb", "aybx", "yaxb", "xayb", "xyab", "yxab", "ayxb", "yxab", "xyab", "axyb", "xyab", "yxab")
GATHER_ORDER = ("bay", "bay", "bay", "bay", "bay", "bay", "bay", "yba", "bay", "yba", "bay", "bay")
SCHEDULE = (
    (0, ((0, 0),)),
    (1, ((1, 0),)),
    (2, ()),
    (3, ((3, 0),)),
    ("result", ((2, 0),)),
    ("down_back0", ()),
    ("down_back1", ((0, 1),)),
    ("down_back2", ((1, 1), (3, 1))),
    ("inner_back0", ()),
    ("inner_back1", ((0, 2),)),
    ("gfn", ()),
    ("handed", ((2, 1),)),
    ("mixed", ((3, 2), (0, 3))),
    (4, ((4, 0), (1, 2))),
    (5, ((5, 0),)),
    (6, ((6, 0),)),
    (7, ((3, 3), (2, 2))),
    (8, ()),
    ("heads0", ((0, 4), (7, 0), (8, 0))),
    ("heads1", ((1, 3),)),
    ("heads2", ((2, 3), (5, 1), (4, 1))),
    (9, ((9, 0),)),
    (10, ((6, 1),)),
    (11, ((3, 4),)),
    ("joint_back", ((0, 5), (2, 4), (10, 0))),
    ("end", (("v", 0), (7, 1), (1, 4), (11, 0), (8, 1), ("v", 1), (4, 2), (9, 1), (5, 2), (3, 5), (6, 2), (0, 6), (2, 5), (1, 5), (4, 3), (10, 1), (5, 3), (11, 1), (3, 6), (2, 6), (8, 2), (1, 6), (4, 4), (5, 4), (7, 2), (0, 7), (8, 3), ("v", 2), (4, 5), (10, 2), (7, 3), (5, 5), (9, 2), (8, 4), (4, 6), (6, 3), (3, 7), (10, 3), (7, 4), (11, 2), (2, 7), (5, 6), (8, 5), (6, 4), (1, 7), (10, 4), (11, 3), ("v", 3), (8, 6), (9, 3), (6, 5), (10, 5), (4, 7), (11, 4), ("v", 4), (7, 5), (9, 4), (6, 6), (5, 7), (10, 6), (11, 5), (8, 7), ("v", 5), (9, 5), (11, 6), (7, 6), (6, 7), (9, 6), (10, 7), (7, 7), (11, 7), (9, 7))),
)
GELU_C = 0.7978845608028654
GELU_A = 0.044715


def aligned(v, by):
    return pl.multiple_of(v, by)


def normal(values):
    average = jnp.mean(values, axis=-1, keepdims=True)
    centered = values - average
    spread = jnp.mean(centered * centered, axis=-1, keepdims=True)
    scale = lax.rsqrt(spread + EPSILON)
    return centered * scale, scale


def normal_back(vhat, scale, gain, grad):
    scaled = grad * gain
    first = jnp.mean(scaled, axis=-1, keepdims=True)
    second = jnp.mean(scaled * vhat, axis=-1, keepdims=True)
    return scale * (scaled - first - vhat * second)


def dot(left, right):
    return jnp.dot(left, right, preferred_element_type=F32)


def dot_t(left, right):
    return lax.dot_general(left, right, (((1,), (1,)), ((), ())), preferred_element_type=F32)


def t_dot(left, right):
    return lax.dot_general(left, right, (((0,), (0,)), ((), ())), preferred_element_type=F32)


def by8(values):
    rows = values.shape[0]
    return jnp.sum(values.reshape(rows // 8, 8, values.shape[1]), axis=0)


class Copies:
    def __init__(self, send, recv):
        self.send, self.recv, self.count, self.open = send, recv, 0, []

    def remote(self, src, dst, device):
        at = self.count
        self.count += 1
        return pltpu.make_async_remote_copy(
            src_ref=src,
            dst_ref=dst,
            send_sem=self.send.at[at],
            recv_sem=self.recv.at[at],
            device_id=device,
            device_id_type=MESH,
        )

    def go(self, src, dst, device, keep=True):
        copy = self.remote(src, dst, device)
        copy.start()
        if keep:
            self.open.append(copy)
        return copy

    def drain(self):
        for copy in self.open:
            copy.wait_send()


class Sums:
    def __init__(self, cp, here, peers, grads, parts, whole, bv, bv_in, deliver):
        self.cp, self.here, self.peers, self.deliver = cp, here, peers, deliver
        self.grads, self.parts, self.whole = grads, parts, whole
        self.bv, self.bv_in, self.copies = bv, bv_in, {}

    def send_part(self, u, k):
        order = SUM_ORDER[u]
        fixed = {axis: self.here[axis] for axis in order[:k]}
        fixed[order[k]] = 1 - self.here[order[k]]
        at = (u,) + tuple(fixed.get(axis, slice(None)) for axis in AXES)
        self.copies[u] = self.cp.go(self.grads.at[at], self.parts[k].at[u], self.peers[order[k]])

    def add_part(self, u, k, **side):
        fixed = {axis: self.here[axis] for axis in SUM_ORDER[u][: k + 1]}
        free = [axis for axis in AXES if axis not in fixed]
        at = (u,) + tuple({**side, **fixed}.get(axis, slice(None)) for axis in AXES)
        part = (u,) + tuple(side.get(axis, slice(None)) for axis in free)
        total = self.grads[at].astype(F32) + self.parts[k][part].astype(F32)
        return at, total.astype(BF16)

    def send_gather(self, u, k):
        order = GATHER_ORDER[u]
        at = (u,) + tuple(
            self.here[axis] if axis in order[k:] else slice(None) for axis in AXES[1:]
        )
        self.copies[u] = self.cp.go(self.whole.at[at], self.whole.at[at], self.peers[order[k]])

    def step(self, u, i):
        if u == "v":
            self.vector(i)
            return
        if i > 0:
            self.copies[u].wait_recv()
        if i == 0:
            self.send_part(u, 0)
        elif i < 4:
            axis = SUM_ORDER[u][i]
            at, total = self.add_part(u, i - 1, **{axis: 1 - self.here[axis]})
            self.grads[at] = total
            self.send_part(u, i)
            at, total = self.add_part(u, i - 1, **{axis: self.here[axis]})
            self.grads[at] = total
        elif i == 4:
            at, total = self.add_part(u, 3)
            self.whole[(u,) + at[2:]] = total
            self.send_gather(u, 0)
        elif i < 7:
            self.send_gather(u, i - 4)
        else:
            self.deliver(u, self.whole.at[u])

    def vector(self, i):
        if i > 0:
            self.copies["v"].wait_recv()
            self.copies["v"].wait_send()
            self.bv[...] += self.bv_in[i - 1]
        if i < 5:
            to = self.peers[("c", *AXES)[i]]
            self.copies["v"] = self.cp.go(self.bv, self.bv_in.at[i], to, keep=False)
        else:
            self.deliver("v", self.bv)


def layer_kernel(
    x_in, cot_in, lens, wj_in, wo_in, wi_in, wd_in,
    *rest,
):
    lines, rest = rest[:13], rest[13:]
    (
    res_out, grad_out, gj_out, go_out, gi_out, gd_out, bv_out,
    wj, wo, wi, wd, feats, cots, ends, normed, q, k, v, vt, kt, bias, pt, scales, mixed_own, mixed,
    sub, fn, handed, tmp, vh, pre, fs, fs_sib, gi_sib, up, gfn, hgr, hg_sib, gmix, do, dqkv,
    result, stat, cols, bv, bv_in, grads, r1, r2, r3, r4, whole,
    vectors, inner_bias, fourth_gain, fourth_bias, *line_refs, lsem, ssem, rsem,
    ) = rest
    R, HD = x_in.shape
    D = 2 * HD
    H = R // 2
    FF = wi.shape[1]
    T = 256
    NT = FF // T
    x = lax.axis_index("section")
    b = lax.axis_index("batch")
    base = (b // GROUP) * GROUP
    z, y, c = (b // 4) % 4, (b // 2) % 2, b % 2
    low, high = z % 2, z // 2

    def dev(x_, z_, y_, c_):
        return (x_, base + z_ * 4 + y_ * 2 + c_)

    sib = dev(x, z, y, 1 - c)
    xp = dev(1 - x, z, y, c)
    xc = dev(1 - x, z, y, 1 - c)
    yp = dev(x, z, 1 - y, c)
    peers = {
        "c": sib, "x": xp, "y": yp,
        "a": dev(x, 2 * high + 1 - low, y, c), "b": dev(x, 2 * (1 - high) + low, y, c),
    }
    home = c == x
    away = c != x
    own = aligned(c * H, 32)
    other = aligned((1 - c) * H, 32)
    cp = Copies(ssem, rsem)
    local_count = [0]

    def local(src, dst):
        copy = pltpu.make_async_copy(src, dst, lsem.at[local_count[0]])
        local_count[0] += 1
        copy.start()
        return copy

    barrier = pltpu.get_barrier_semaphore()
    for peer in (*peers.values(), xc):
        pl.semaphore_signal(barrier, inc=1, device_id=peer, device_id_type=MESH)

    line_refs += [inner_bias, fourth_gain, fourth_bias]
    line_copies = [local(src, dst) for src, dst in zip(lines, line_refs)]
    (
        first_gain, first_bias, query_bias, value_bias, second_gain, second_bias, output_bias,
        third_gain, third_bias, down_bias,
    ) = (vectors.at[i : i + 1] for i in range(10))

    @pl.when(home)
    def _():
        lane = lax.broadcasted_iota(jnp.int32, (1, 8), 1)
        lengths = lens[...].astype(F32)
        for j in range(8):
            end = jnp.sum(jnp.where(lane <= j, lengths, 0.0), axis=1, keepdims=True)
            ends[j : j + 1, :] = jnp.broadcast_to(end, (1, 128))

    pl.semaphore_wait(barrier, 6)

    NC = 3
    RC = R // NC
    c_native = [cp.remote(src, dst.at[x], sib) for src, dst in ((x_in, feats), (cot_in, cots))]
    c_ends = cp.remote(ends, ends, sib)
    c_cross = [
        cp.remote(x_in.at[pl.ds(i * RC, RC)], feats.at[x, pl.ds(i * RC, RC)], xp) for i in range(NC)
    ]
    c_pass = [
        cp.remote(feats.at[1 - x, pl.ds(i * RC, RC)], feats.at[1 - x, pl.ds(i * RC, RC)], sib)
        for i in range(NC)
    ]
    cot_cross = cp.remote(cot_in, cots.at[x], xp)
    cot_pass = cp.remote(cots.at[1 - x], cots.at[1 - x], sib)
    l_native = [
        pltpu.make_async_copy(src, dst.at[x], lsem.at[44 + i])
        for i, (src, dst) in enumerate(((x_in, feats), (cot_in, cots)))
    ]

    @pl.when(away)
    def _():
        c_cross[0].start()
        c_cross[1].start()

    @pl.when(home)
    def _():
        c_native[0].start()
        l_native[0].start()
        c_ends.start()
        l_native[1].start()
        c_native[1].start()
        l_native[0].wait()

    wj_copies = [local(wj_in.at[:, pl.ds(aligned(t * D + c * HD, 128), HD)], wj.at[t]) for t in range(3)]
    wo_copy = local(wo_in, wo)
    wi_copy = local(wi_in, wi)
    wd_copy = local(wd_in, wd)

    @pl.when(away)
    def _():
        c_native[0].wait_recv()
        c_ends.wait_recv()

    for copy in line_copies:
        copy.wait()
    for i in range(10):
        vectors[i : i + 1, :] = line_refs[i][...].reshape(1, D)
    zeros = jnp.zeros((640 - R, HD), BF16)
    for ref in (q, do):
        ref[R:640, :] = zeros

    key_at = lax.broadcasted_iota(jnp.int32, (R, 128), 0).astype(F32)
    key_segment = sum((key_at >= ends[j : j + 1, :]).astype(F32) for j in range(8))
    for j in range(5):
        query_at = (lax.broadcasted_iota(jnp.int32, (1, 128), 1) + j * 128).astype(F32)
        query_segment = sum((query_at >= ends[i : i + 1, :]).astype(F32) for i in range(8))
        allowed = (key_segment == query_segment) & (key_at <= query_at)
        bias[:, j * 128 : (j + 1) * 128] = jnp.where(allowed, 0.0, MASKED).astype(BF16)

    def feature_rows(at, count):
        return jnp.concatenate([feats[0, pl.ds(at, count)], feats[1, pl.ds(at, count)]], 1).astype(F32)

    for copy in wj_copies:
        copy.wait()
    heads_at = aligned(c * HD, 128)
    own_query_bias = query_bias[:, pl.ds(heads_at, HD)]
    own_value_bias = value_bias[:, pl.ds(heads_at, HD)]
    for i in range(NC):

        @pl.when(home)
        def _():
            c_cross[i].wait_recv()
            c_pass[i].start()

        @pl.when(away)
        def _():
            if i == 0:
                c_cross[0].wait_send()
                c_cross[2].start()
            if i == 1:
                c_cross[1].wait_send()
                c_cross[2].wait_send()
                cot_cross.start()
            c_pass[i].wait_recv()

        @pl.loop(0, RC // 48)
        def _(step):
            at = aligned(i * RC + step * 48, 16)
            vhat, _ = normal(feature_rows(at, 48))
            normed[pl.ds(at, 48), :] = (vhat * first_gain[...] + first_bias[...]).astype(BF16)

        rows = normed[i * RC : (i + 1) * RC, :]
        at = pl.ds(i * RC, RC)
        q[at, :] = ((dot(rows, wj[0]) + own_query_bias).astype(BF16) * 0.125).astype(BF16)
        k[at, :] = dot(rows, wj[1]).astype(BF16)
        v[at, :] = (dot(rows, wj[2]) + own_value_bias).astype(BF16)
    vt[:, :R] = v[...].T

    first_half = lax.broadcasted_iota(jnp.int32, (128, 128), 1) < 64

    def split_pair(tile):
        zero = jnp.zeros_like(tile)
        return jnp.concatenate([jnp.where(first_half, tile, zero), jnp.where(first_half, zero, tile)], 0)

    blocks = []
    at = 0
    for j in range(5):
        blocks.append((j, min(128 * (j + 1), R), at))
        at += min(128 * (j + 1), R)
    c_mixed = []
    for pr in range(PAIRS):
        lanes = slice(pr * 128, (pr + 1) * 128)
        for j, nk, at in blocks:
            qs = slice(j * 128, (j + 1) * 128)
            block_bias = bias[:nk, qs].astype(F32)
            scores = dot_t(k[:nk, lanes], split_pair(q[qs, lanes]))
            scores = scores + jnp.concatenate([block_bias, block_bias], 1)
            largest = jnp.max(scores, axis=0, keepdims=True)
            shifted = jnp.exp(scores - largest)
            summed = jnp.sum(shifted, axis=0, keepdims=True)
            scale = 1.0 / summed
            weights = shifted.astype(BF16)
            pt[pr, at : at + nk, :] = weights
            scales[pr * 5 + j] = jnp.broadcast_to(scale, (8, 256))
            out = dot(vt[lanes, :nk], weights) * scale
            mixed_own[qs, lanes] = jnp.concatenate([out[:64, :128], out[64:, 128:]], 0).T
        there = pl.ds(aligned(c * HD + pr * 128, 128), 128)
        c_mixed.append(cp.go(mixed_own.at[pl.ds(other, H), lanes], mixed.at[:, there], sib))
        mixed[:, there] = mixed_own[pl.ds(own, H), lanes]

    kt[:, :R] = k[...].T

    @pl.when(home)
    def _():
        cot_cross.wait_recv()
        cot_pass.start()
        l_native[1].wait()
        cot_pass.wait_send()

    @pl.when(away)
    def _():
        c_native[1].wait_recv()
        cot_pass.wait_recv()

    @pl.loop(0, R // 48)
    def _(step):
        at = aligned(step * 48, 16)
        alive = (lax.broadcasted_iota(jnp.int32, (48, 1), 0) + at).astype(F32) < ends[7:8, 0:1]
        for h in range(2):
            rows = cots[h, pl.ds(at, 48), :].astype(F32)
            cots[h, pl.ds(at, 48), :] = jnp.where(alive, rows, 0.0).astype(BF16)

    up[:, :HD] = cots[0, pl.ds(own, H), :]
    up[:, HD:] = cots[1, pl.ds(own, H), :]

    wo_copy.wait()
    for copy in c_mixed:
        copy.wait_recv()
    own_live = (lax.broadcasted_iota(jnp.int32, (H, 1), 0) + c * H).astype(F32) < ends[7:8, 0:1]

    @pl.loop(0, H // 48)
    def _(step):
        at = aligned(step * 48, 16)
        vhat, _ = normal(mixed[pl.ds(at, 48), :])
        sub[pl.ds(own + at, 48), :] = (vhat * second_gain[...] + second_bias[...]).astype(BF16)

    branch = dot(sub[pl.ds(own, H), :], wo[...])
    for i in range(6):
        piece = slice(i * 48, (i + 1) * 48)
        handed[piece, :] = (
            feature_rows(own + i * 48, 48) + (branch[piece] + output_bias[...])
        ).astype(BF16)
        vhat, _ = normal(handed[piece, :].astype(F32))
        fn[pl.ds(own + i * 48, 48), :] = (vhat * third_gain[...] + third_bias[...]).astype(BF16)
    c_sub = cp.go(sub.at[pl.ds(own, H)], sub.at[pl.ds(own, H)], sib)
    c_fn = cp.go(fn.at[pl.ds(own, H)], fn.at[pl.ds(own, H)], sib)

    wi_copy.wait()

    def feed_dot(tile):
        at = pl.ds(aligned(tile * T, T), T)
        tmp[:, at] = dot(fn[pl.ds(own, H), :], wi[:, at])

    def feed_tile(tile, first=False):
        at = pl.ds(aligned(tile * T, T), T)
        for i in range(9):
            piece = slice(i * 32, (i + 1) * 32)
            u = tmp[piece, at] + inner_bias[:, at]
            pre[piece, at] = u.astype(BF16)
            half = 0.5 * u
            act = half + half * jnp.tanh(u * (GELU_C + (GELU_C * GELU_A) * (u * u)))
            tmp[piece, at] = act
            if first:
                near = jnp.sum(act, axis=1, keepdims=True) * (1.0 / T)
                stat[1, piece, :] = jnp.broadcast_to(near, (32, 128))
            near = stat[1, piece, :]
            low, high = act[:, :128] - near, act[:, 128:] - near
            if first:
                stat[0, piece, :] = low + high
                stat[2, piece, :] = low * low + high * high
            else:
                stat[0, piece, :] += low + high
                stat[2, piece, :] += low * low + high * high

    feed_dot(0)
    feed_dot(1)
    feed_tile(0, True)

    @pl.loop(1, NT - 1)
    def _(tile):
        feed_dot(tile + 1)
        feed_tile(tile)

    feed_tile(NT - 1)
    shift = jnp.sum(stat[0], axis=1, keepdims=True) * (1.0 / FF)
    spread = jnp.sum(stat[2], axis=1, keepdims=True) * (1.0 / FF) - shift * shift
    stat[1] = stat[1] + shift
    stat[2] = jnp.broadcast_to(lax.rsqrt(jnp.maximum(spread, 0.0) + EPSILON), (H, 128))

    def feed_norm(block):
        at = pl.ds(aligned(block * HD, HD), HD)
        for i in range(9):
            piece = slice(i * 32, (i + 1) * 32)
            m, s = stat[1, piece, :], stat[2, piece, :]
            vhat = (tmp[piece, at] - jnp.concatenate([m, m, m], 1)) * jnp.concatenate([s, s, s], 1)
            vh[piece, at] = vhat.astype(BF16)
            fs[piece, at] = (vhat * fourth_gain[:, at] + fourth_bias[:, at]).astype(BF16)

    c_fs = []
    for part in range(2):
        for i in range(2):
            feed_norm(4 * i + 2 * (1 - c) + part)
        for i in range(2):
            c_fs.append(
                cp.go(
                    fs.at[:, pl.ds(aligned((4 * i + 2 * (1 - c) + part) * HD, 128), HD)],
                    fs_sib.at[:, (2 * i + part) * HD : (2 * i + part + 1) * HD],
                    sib,
                    keep=False,
                )
            )

    @pl.loop(0, 4)
    def _(step):
        feed_norm((step // 2) * 4 + 2 * c + step % 2)

    deliveries = []

    def deliver(u, total):
        if u == "v":
            deliveries.append((None, local(total, bv_out)))
            return
        rows = (slice(None),) * 4
        if u < 4:
            target = gd_out.at[(c, u // 2) + rows + (slice((u % 2) * HD, (u % 2 + 1) * HD),)]
        elif u < 8:
            target = gi_out.at[rows + (pl.ds(aligned(c * (FF // 2) + (u - 4) * HD, 128), HD),)]
        elif u == 8:
            target = go_out.at[rows + (pl.ds(heads_at, HD),)]
        else:
            target = gj_out.at[rows + (pl.ds(aligned((u - 9) * D + c * HD, 128), HD),)]
        deliveries.append((cp.go(total, target, sib), local(total, target)))

    here = {"x": x, "y": y, "a": low, "b": high}
    sums = Sums(cp, here, peers, grads, (r1, r2, r3, r4), whole, bv, bv_in, deliver)
    schedule = iter(SCHEDULE)

    def pump(mark):
        at, steps = next(schedule)
        assert at == mark
        for u, i in steps:
            sums.step(u, i)


    def cut_rows(unit):
        return unit.astype(BF16).reshape(2, 2, 2, HD // 8, HD)

    def units(first, count, left_own, left_sib, right):
        for i in range(count):
            if first == 0 and i % 2 == 0:
                c_fs[i].wait_recv()
                c_fs[i + 1].wait_recv()
            for h in range(2):
                rows = jnp.concatenate([left_own(i, h), left_sib(i, h)], 0)
                grads[first + i, h] = cut_rows(t_dot(rows, right(i)))
            pump(first + i)

    units(
        0, 4,
        lambda i, h: fs[:, pl.ds(aligned((2 * h + c) * D + (i // 2) * HD, 128), HD)],
        lambda i, h: fs_sib[:, h * D + (i // 2) * HD : h * D + (i // 2 + 1) * HD],
        lambda i: jnp.concatenate([cots[i % 2, pl.ds(own, H), :], cots[i % 2, pl.ds(other, H), :]], 0),
    )

    wd_copy.wait()
    c_result = [
        cp.remote(result.at[0, x], res_out.at[pl.ds(own, H)], sib),
        cp.remote(result.at[0, 1 - x], res_out.at[pl.ds(own, H)], xp),
        cp.remote(result.at[0, 1 - x], res_out.at[pl.ds(own, H)], xc),
        cp.remote(result.at[1, x], grad_out.at[pl.ds(own, H)], sib),
        cp.remote(result.at[1, 1 - x], grad_out.at[pl.ds(own, H)], xp),
        cp.remote(result.at[1, 1 - x], grad_out.at[pl.ds(own, H)], xc),
    ]
    l_result = [
        pltpu.make_async_copy(result.at[i, x], o.at[pl.ds(own, H)], lsem.at[46 + i])
        for i, o in enumerate((res_out, grad_out))
    ]

    def hand_out(i):
        @pl.when(home)
        def _():
            l_result[i].start()
            c_result[3 * i + 1].start()

        @pl.when(away)
        def _():
            c_result[3 * i].start()
            c_result[3 * i + 2].start()

    def handed_out(i):
        @pl.when(home)
        def _():
            l_result[i].wait()
            c_result[3 * i + 1].wait_send()
            c_result[3 * i].wait_recv()

        @pl.when(away)
        def _():
            c_result[3 * i].wait_send()
            c_result[3 * i + 2].wait_send()
            c_result[3 * i + 1].wait_recv()
            c_result[3 * i + 2].wait_recv()

    branch = dot(fs[...], wd[...])
    for i in range(6):
        piece = slice(i * 48, (i + 1) * 48)
        alive = own_live[piece]
        rows = handed[piece, :].astype(F32) + (branch[piece] + down_bias[...])
        rows = jnp.where(alive, rows, 0.0).astype(BF16)
        result[0, 0, piece, :] = rows[:, :HD]
        result[0, 1, piece, :] = rows[:, HD:]
    hand_out(0)
    pump("result")

    stat[0] = jnp.zeros((H, 128), F32)
    stat[1] = jnp.zeros((H, 128), F32)

    def down_back(tile):
        at = pl.ds(aligned(tile * T, T), T)
        grad = dot_t(up[...], wd[at, :])
        total_gain = jnp.zeros((8, T), F32)
        total_bias = jnp.zeros((8, T), F32)
        for i in range(9):
            piece = slice(i * 32, (i + 1) * 32)
            g = grad[piece]
            vhat = vh[piece, at].astype(F32)
            tmp[piece, at] = g
            gv = g * vhat
            total_gain += by8(gv)
            total_bias += by8(g)
            gain = fourth_gain[:, at]
            g, gv = g * gain, gv * gain
            stat[0, piece, :] += g[:, :128] + g[:, 128:]
            stat[1, piece, :] += gv[:, :128] + gv[:, 128:]
        cols[0, tile] = total_gain
        cols[1, tile] = total_bias

    for i in range(3):
        pl.loop(i * NT // 3, (i + 1) * NT // 3)(down_back)
        pump(f"down_back{i}")

    for i in range(2):
        mean = jnp.sum(stat[i], axis=1, keepdims=True) * (1.0 / FF)
        stat[i] = jnp.broadcast_to(mean, (H, 128))
    for copy in c_fs:
        copy.wait_send()
    gi = fs

    def inner_back(tile):
        at = pl.ds(aligned(tile * T, T), T)
        total = jnp.zeros((8, T), F32)
        for i in range(9):
            piece = slice(i * 32, (i + 1) * 32)
            m1, m2, s = stat[0, piece, :], stat[1, piece, :], stat[2, piece, :]
            vhat = vh[piece, at].astype(F32)
            grad = tmp[piece, at] * fourth_gain[:, at] - jnp.concatenate([m1, m1], 1)
            grad = (grad - vhat * jnp.concatenate([m2, m2], 1)) * jnp.concatenate([s, s], 1)
            u = pre[piece, at].astype(F32)
            square = u * u
            t = jnp.tanh(u * (GELU_C + (GELU_C * GELU_A) * square))
            half = 0.5 * u
            slope = 0.5 + 0.5 * t + (half - half * t * t) * (
                GELU_C + (3 * GELU_C * GELU_A) * square
            )
            low = (grad * slope).astype(BF16)
            gi[piece, at] = low
            total += by8(low.astype(F32))
        cols[2, tile] = total

    for i in range(2):
        pl.loop(i * NT // 2, (i + 1) * NT // 2)(inner_back)
        pump(f"inner_back{i}")

    c_gi = cp.go(gi.at[:, pl.ds(aligned((1 - c) * (FF // 2), 128), FF // 2)], gi_sib, sib)
    gfn[...] = dot_t(gi[...], wi[...])
    pump("gfn")

    total_gain = jnp.zeros((8, D), F32)
    total_bias = jnp.zeros((8, D), F32)
    total_out = jnp.zeros((8, D), F32)
    for i in range(6):
        piece = slice(i * 48, (i + 1) * 48)
        vhat, scale = normal(handed[piece, :].astype(F32))
        grad = gfn[piece, :]
        total_gain += by8(grad * vhat)
        total_bias += by8(grad)
        low = (
            up[piece, :].astype(F32) + normal_back(vhat, scale, third_gain[...], grad)
        ).astype(BF16)
        hgr[piece, :] = low
        total_out += by8(low.astype(F32))

    def store_vector(row, total):
        bv[row : row + 1, :] = jnp.sum(total, axis=0, keepdims=True)

    store_vector(6, total_out)
    store_vector(7, total_gain)
    store_vector(8, total_bias)
    c_hg = cp.go(hgr.at[:, pl.ds(aligned((1 - c) * HD, 128), HD)], hg_sib, sib)

    pump("handed")

    gfn[...] = dot_t(hgr[...], wo[...])
    total_gain = jnp.zeros((8, D), F32)
    total_bias = jnp.zeros((8, D), F32)
    for i in range(6):
        piece = slice(i * 48, (i + 1) * 48)
        vhat, scale = normal(mixed[piece, :])
        grad = gfn[piece, :]
        total_gain += by8(grad * vhat)
        total_bias += by8(grad)
        gmix[piece, :] = normal_back(vhat, scale, second_gain[...], grad).astype(BF16)
    store_vector(4, total_gain)
    store_vector(5, total_bias)
    c_gmix = cp.go(
        gmix.at[:, pl.ds(aligned((1 - c) * HD, 128), HD)], do.at[pl.ds(own, H)], sib
    )
    do[pl.ds(own, H), :] = gmix[:, pl.ds(heads_at, HD)]

    pump("mixed")

    c_fn.wait_recv()
    c_gi.wait_recv()

    def fn_rows(at):
        return lambda i, h: fn[pl.ds(at, H), h * HD : (h + 1) * HD]

    units(
        4, 4, fn_rows(own), fn_rows(other),
        lambda i: jnp.concatenate(
            [gi[:, pl.ds(aligned(c * (FF // 2) + i * HD, 128), HD)], gi_sib[:, i * HD : (i + 1) * HD]], 0
        ),
    )
    c_sub.wait_recv()
    c_hg.wait_recv()

    def sub_rows(at):
        return lambda i, h: sub[pl.ds(at, H), h * HD : (h + 1) * HD]

    units(
        8, 1, sub_rows(own), sub_rows(other),
        lambda i: jnp.concatenate([hgr[:, pl.ds(heads_at, HD)], hg_sib[...]], 0),
    )

    c_gmix.wait_recv()
    for pr in range(PAIRS):
        lanes = slice(pr * 128, (pr + 1) * 128)
        for j, nk, at in reversed(blocks):
            qs = slice(j * 128, (j + 1) * 128)
            exact = pt[pr, at : at + nk, :].astype(F32) * scales[pr * 5 + j][:1]
            probs = exact.astype(BF16)
            do_split = split_pair(do[qs, lanes])
            grad_probs = dot_t(v[:nk, lanes], do_split)
            inner_sum = jnp.sum(exact * grad_probs, axis=0, keepdims=True)
            grad_scores = (exact * (grad_probs - inner_sum)).astype(BF16)
            value_part = dot(probs, do_split)
            key_part = dot(grad_scores, split_pair(q[qs, lanes]))
            if j == len(blocks) - 1:
                gfn[:, :128] = value_part[:H]
                gfn[:, 128:256] = value_part[H:]
                gfn[:, 256:384] = key_part[:H]
                gfn[:, 384:512] = key_part[H:]
            else:
                for lane_at, part in ((0, value_part), (256, key_part)):
                    top = min(nk, H)
                    gfn[:top, lane_at : lane_at + 128] += part[:top]
                    if nk > H:
                        gfn[: nk - H, lane_at + 128 : lane_at + 256] += part[H:]
            out = dot(kt[lanes, :nk], grad_scores)
            query_part = jnp.concatenate([out[:64, :128], out[64:, 128:]], 0).T * 0.125
            count = min(128, R - j * 128)
            dqkv[j * 128 : j * 128 + count, lanes] = query_part[:count].astype(BF16)
        for half in range(2):
            rows = slice(half * H, (half + 1) * H)
            dqkv[rows, 2 * HD + pr * 128 : 2 * HD + (pr + 1) * 128] = gfn[
                :, half * 128 : (half + 1) * 128
            ].astype(BF16)
            dqkv[rows, HD + pr * 128 : HD + (pr + 1) * 128] = gfn[
                :, 256 + half * 128 : 256 + (half + 1) * 128
            ].astype(BF16)
        pump(f"heads{pr}")

    for i in range(3):
        for h in range(2):
            grads[9 + i, h] = cut_rows(
                t_dot(normed[:, h * HD : (h + 1) * HD], dqkv[:, i * HD : (i + 1) * HD])
            )
        pump(9 + i)
    bv[2:4, :] = jnp.zeros((2, D), F32)
    for row, at in ((2, 0), (3, 2 * HD)):
        total = jnp.zeros((8, HD), F32)
        for i in range(12):
            total += by8(dqkv[i * 48 : (i + 1) * 48, at : at + HD].astype(F32))
        bv[row : row + 1, pl.ds(heads_at, HD)] = jnp.sum(total, axis=0, keepdims=True)

    for part, at in ((0, other), (1, own)):
        total = jnp.zeros((H, D), F32)
        for i in range(3):
            total += dot_t(dqkv[pl.ds(at, H), i * HD : (i + 1) * HD], wj[i])
        tmp[:, part * D : (part + 1) * D] = total
        if part == 0:
            c_gn = cp.go(tmp.at[:, :D], mixed, sib)
    c_gn.wait_recv()
    pump("joint_back")
    total_gain = jnp.zeros((8, D), F32)
    total_bias = jnp.zeros((8, D), F32)
    total_down = jnp.zeros((8, D), F32)
    for i in range(6):
        piece = slice(i * 48, (i + 1) * 48)
        vhat, scale = normal(feature_rows(own + i * 48, 48))
        grad = tmp[piece, D : 2 * D] + mixed[piece, :]
        total_gain += by8(grad * vhat)
        total_bias += by8(grad)
        total_down += by8(up[piece, :].astype(F32))
        rows = (
            hgr[piece, :].astype(F32) + normal_back(vhat, scale, first_gain[...], grad)
        ).astype(BF16)
        result[1, 0, piece, :] = rows[:, :HD]
        result[1, 1, piece, :] = rows[:, HD:]
    hand_out(1)
    store_vector(0, total_gain)
    store_vector(1, total_bias)
    store_vector(9, total_down)
    for kind, row in ((2, 10), (0, 14), (1, 18)):
        for tile in range(NT):
            bv[row + tile // 3 : row + tile // 3 + 1, (tile % 3) * T : (tile % 3 + 1) * T] = jnp.sum(
                cols[kind, tile], axis=0, keepdims=True
            )
    bv[22:24, :] = jnp.zeros((2, D), F32)

    pump("end")

    @pl.when(home)
    def _():
        for copy in c_native + [c_ends] + c_pass:
            copy.wait_send()

    @pl.when(away)
    def _():
        cot_cross.wait_send()

    handed_out(0)
    handed_out(1)
    for copy, here in deliveries:
        if copy is not None:
            copy.wait_recv()
        here.wait()
    cp.drain()


def finish_kernel(gj, go, gi, gd, bv, res, grad, oj, oo, oi, od, *rest):
    *vectors, res_out, grad_out = rest

    @pl.when(pl.program_id(0) == 0)
    def _():
        x = lax.axis_index("section")
        HD = oo.shape[1] // 2
        at = pl.ds(aligned(x * HD, 128), HD)
        for row in range(10):
            vectors[row][...] = bv[row : row + 1, at].reshape(HD)
        for i in range(3):
            row = 10 + 4 * i
            halves = [jnp.concatenate([bv[j : j + 1, :], bv[j + 1 : j + 2, :]], 1) for j in (row, row + 2)]
            vectors[10 + i][...] = jnp.where(x == 0, *halves).reshape(4 * HD)

    oj[...] = gj[...].astype(F32)
    oo[...] = go[...].astype(F32)
    oi[...] = gi[...].astype(F32)
    od[...] = gd[...].astype(F32)

    res_out[...] = res[...]
    grad_out[...] = grad[...]


def per_device(
    inputs, seq_lengths, cotangent,
    first_gain, first_bias, joint_weight, query_bias, value_bias, second_gain, second_bias,
    output_weight, output_bias, third_gain, third_bias, inner_weight, inner_bias,
    fourth_gain, fourth_bias, down_weight, down_bias,
):
    R, HD = inputs.shape
    D, H, FF = 2 * HD, R // 2, inner_weight.shape[1]
    hbm = pl.BlockSpec(memory_space=pl.ANY)
    vmem = pl.BlockSpec(memory_space=pltpu.VMEM)
    lines = (
        first_gain, first_bias, query_bias, value_bias, second_gain, second_bias, output_bias,
        third_gain, third_bias, down_bias,
    )
    lines += tuple(m.reshape(1, -1) for m in (inner_bias, fourth_gain, fourth_bias))
    V = pltpu.VMEM
    scratch = [
        V((3, D, HD), BF16), V((D, D), BF16), V((D, FF), BF16), V((FF, D), BF16),
        V((2, R, HD), BF16), V((2, R, HD), BF16), V((8, 128), F32), V((R, D), BF16),
        V((640, HD), BF16), V((R, HD), BF16), V((R, HD), BF16),
        V((HD, 640), BF16), V((HD, 640), BF16), V((R, 640), BF16),
        V((PAIRS, 128 * 10 + R, 256), BF16), V((PAIRS * 5, 8, 256), F32),
        V((640, HD), F32), V((H, D), F32),
        V((R, D), BF16), V((R, D), BF16), V((H, D), BF16),
        V((H, FF), F32), V((H, FF), BF16), V((H, FF), BF16),
        V((H, FF), BF16), V((H, FF // 2), BF16), V((H, FF // 2), BF16),
        V((H, D), BF16), V((H, D), F32), V((H, D), BF16), V((H, HD), BF16),
        V((H, D), BF16), V((640, HD), BF16), V((R, 3 * HD), BF16),
        V((2, 2, H, HD), BF16), V((3, H, 128), F32),
        V((3, FF // 256, 8, 256), F32), V((24, D), F32), V((5, 24, D), F32),
        V((UNITS, 2, 2, 2, 2, HD // 8, HD), BF16),
        V((UNITS, 2, 2, 2, HD // 8, HD), BF16), V((UNITS, 2, 2, HD // 8, HD), BF16),
        V((UNITS, 2, HD // 8, HD), BF16), V((UNITS, HD // 8, HD), BF16),
        V((UNITS, 2, 2, 2, HD // 8, HD), BF16),
        V((10, D), F32), *[V((1, FF), F32)] * 3, *[V((D,), F32)] * 10,
        pltpu.SemaphoreType.DMA((48,)), pltpu.SemaphoreType.DMA((200,)), pltpu.SemaphoreType.DMA((200,)),
    ]
    shape = jax.ShapeDtypeStruct
    result, input_grad, gj, go, gi, gd, bv = pl.pallas_call(
        layer_kernel,
        out_shape=[
            shape((R, HD), BF16), shape((R, HD), BF16),
            *(shape((2, 2, 2, HD // 8, n), BF16) for n in (3 * D, D, FF)),
            shape((2, 2, 2, 2, 2, HD // 8, D), BF16), shape((24, D), F32),
        ],
        in_specs=[hbm, hbm, vmem, hbm, hbm, hbm, hbm] + [hbm] * 13,
        out_specs=[hbm] * 7,
        scratch_shapes=scratch,
        compiler_params=pltpu.CompilerParams(
            collective_id=0, has_side_effects=True, vmem_limit_bytes=66_000_000
        ),
        cost_estimate=pl.CostEstimate(flops=16 * 10**9, bytes_accessed=25 * 10**6, transcendentals=4 * 10**6),
    )(inputs, cotangent, seq_lengths, joint_weight, output_weight, inner_weight, down_weight, *lines)
    steps = 2
    wide = [(HD, 3 * D), (HD, D), (HD, FF), (FF // 2, D)]
    gj, go, gi, gd = (m.reshape(s) for m, s in zip((gj, go, gi, gd), wide))

    def block(rows, columns):
        return pl.BlockSpec((rows // steps, columns), lambda i: (i, 0))

    small = [(HD,)] * 10 + [(FF // 2,)] * 3
    groups = lax.axis_size("batch") // GROUP
    if groups > 1:
        peers = [[r + GROUP * g for g in range(groups)] for r in range(GROUP)]
        gj, go, gi, gd, bv = lax.psum(
            tuple(m.astype(F32) for m in (gj, go, gi, gd, bv)), "batch", axis_index_groups=peers
        )
    outs = pl.pallas_call(
        finish_kernel,
        grid=(steps,),
        out_shape=[shape(s, F32) for s in wide + small] + [shape((R, HD), BF16)] * 2,
        in_specs=[block(*s) for s in wide] + [pl.BlockSpec((24, D), lambda i: (0, 0))] + [block(R, HD)] * 2,
        out_specs=[block(*s) for s in wide] + [pl.BlockSpec(s, lambda i: (0,)) for s in small] + [block(R, HD)] * 2,
        compiler_params=pltpu.CompilerParams(vmem_limit_bytes=66_000_000),
    )(gj, go, gi, gd, bv, result, input_grad)
    result, input_grad = outs[-2:]
    dj, dout, di, dd = outs[:4]
    fg, fb, qb, vb, sg, sb, ob, tg, tb, db, ib, hg, hb = outs[4:-2]
    return (
        result, input_grad, fg, fb, dj, qb, vb, sg, sb, dout, ob, tg, tb, di, ib, hg, hb, dd, db,
    )


def solution(mesh):
    wide = P("section", None)
    line = P("section")
    return jax.shard_map(
        per_device,
        mesh=mesh,
        in_specs=(P("batch", "section"), P("batch", None), P("batch", "section")) + (P(),) * 17,
        out_specs=(
            P("batch", "section"), P("batch", "section"), line, line, wide, line, line, line, line,
            wide, line, line, line, wide, line, line, line, wide, line,
        ),
        check_vma=False,
    )
```

```python
import functools

import jax
import jax.numpy as jnp
from jax import lax
from jax.experimental import pallas as pl
from jax.experimental.pallas import tpu as pltpu
from jax.sharding import PartitionSpec as P

HEADS = 12
EPSILON = 1e-05
MASKED = -1e9
F32 = jnp.float32
BF16 = jnp.bfloat16
MESH = pl.DeviceIdType.MESH
GROUP = 16
PAIRS = HEADS // 4
UNITS = 12
AXES = ("x", "y", "a", "b")
SUM_ORDER = ("yabx", "yaxb", "xayb", "ayxb", "xyab", "yabx", "yxab", "axyb", "xayb", "xyab", "yxab", "yxab")
GATHER_ORDER = ("bay", "bay", "bay", "bay", "bay", "bya", "bay", "bya", "bay", "bay", "bya", "bay")
SCHEDULE = (
    (0, ((0, 0),)),
    (1, ()),
    (2, ((2, 0),)),
    (3, ((1, 0), (3, 0))),
    ("result", ()),
    ("down_back0", ()),
    ("down_back1", ()),
    ("down_back2", ()),
    ("inner_back0", ()),
    ("inner_back1", ((0, 1),)),
    ("gfn", ((2, 1),)),
    ("handed", ((3, 1),)),
    ("mixed", ()),
    (4, ((4, 0),)),
    (5, ((5, 0),)),
    (6, ((1, 1), (0, 2))),
    (7, ((7, 0),)),
    (8, ((8, 0),)),
    ("heads0", ((2, 2), (3, 2), (6, 0))),
    ("heads1", ((1, 2),)),
    ("heads2", ((4, 1), (0, 3))),
    (9, ((5, 1),)),
    (10, ()),
    (11, ((9, 0),)),
    ("joint_back", ((2, 3),)),
    ("end", ((8, 1), (7, 1), (3, 3), (10, 0), ("v", 0), (1, 3), (5, 2), (6, 1), (0, 4), ("v", 1), (2, 4), (11, 0), (4, 2), (8, 2), (3, 4), (1, 4), (9, 1), (5, 3), (0, 5), (10, 1), (4, 3), (2, 5), (3, 5), (0, 6), (1, 5), (7, 2), (4, 4), (2, 6), (11, 1), (3, 6), (6, 2), (8, 3), (1, 6), ("v", 2), (5, 4), (4, 5), (9, 2), (6, 3), (8, 4), (10, 2), (0, 7), (4, 6), (5, 5), (7, 3), (9, 3), (11, 2), (6, 4), (8, 5), (2, 7), (10, 3), (7, 4), (9, 4), (3, 7), (11, 3), (6, 5), (8, 6), (1, 7), (10, 4), ("v", 3), (7, 5), (9, 5), (6, 6), (11, 4), (4, 7), (10, 5), (5, 6), ("v", 4), (9, 6), (8, 7), (11, 5), (7, 6), (5, 7), (6, 7), ("v", 5), (11, 6), (10, 6), (7, 7), (9, 7), (10, 7), (11, 7))),
)
GELU_C = 0.7978845608028654
GELU_A = 0.044715


def aligned(v, by):
    return pl.multiple_of(v, by)


def normal(values):
    average = jnp.mean(values, axis=-1, keepdims=True)
    centered = values - average
    spread = jnp.mean(centered * centered, axis=-1, keepdims=True)
    scale = lax.rsqrt(spread + EPSILON)
    return centered * scale, scale


def normal_back(vhat, scale, gain, grad):
    scaled = grad * gain
    first = jnp.mean(scaled, axis=-1, keepdims=True)
    second = jnp.mean(scaled * vhat, axis=-1, keepdims=True)
    return scale * (scaled - first - vhat * second)


def dot(left, right):
    return jnp.dot(left, right, preferred_element_type=F32)


def dot_t(left, right):
    return lax.dot_general(left, right, (((1,), (1,)), ((), ())), preferred_element_type=F32)


def t_dot(left, right):
    return lax.dot_general(left, right, (((0,), (0,)), ((), ())), preferred_element_type=F32)


def by8(values):
    rows = values.shape[0]
    return jnp.sum(values.reshape(rows // 8, 8, values.shape[1]), axis=0)


class Copies:
    def __init__(self, send, recv):
        self.send, self.recv, self.count, self.open = send, recv, 0, []

    def remote(self, src, dst, device):
        at = self.count
        self.count += 1
        return pltpu.make_async_remote_copy(
            src_ref=src,
            dst_ref=dst,
            send_sem=self.send.at[at],
            recv_sem=self.recv.at[at],
            device_id=device,
            device_id_type=MESH,
        )

    def go(self, src, dst, device, keep=True):
        copy = self.remote(src, dst, device)
        copy.start()
        if keep:
            self.open.append(copy)
        return copy

    def drain(self):
        for copy in self.open:
            copy.wait_send()


class Sums:
    def __init__(self, cp, here, peers, grads, parts, whole, bv, bv_in, deliver):
        self.cp, self.here, self.peers, self.deliver = cp, here, peers, deliver
        self.grads, self.parts, self.whole = grads, parts, whole
        self.bv, self.bv_in, self.copies = bv, bv_in, {}

    def send_part(self, u, k):
        order = SUM_ORDER[u]
        fixed = {axis: self.here[axis] for axis in order[:k]}
        fixed[order[k]] = 1 - self.here[order[k]]
        at = (u,) + tuple(fixed.get(axis, slice(None)) for axis in AXES)
        self.copies[u] = self.cp.go(self.grads.at[at], self.parts[k].at[u], self.peers[order[k]])

    def add_part(self, u, k, **side):
        fixed = {axis: self.here[axis] for axis in SUM_ORDER[u][: k + 1]}
        free = [axis for axis in AXES if axis not in fixed]
        at = (u,) + tuple({**side, **fixed}.get(axis, slice(None)) for axis in AXES)
        part = (u,) + tuple(side.get(axis, slice(None)) for axis in free)
        total = self.grads[at].astype(F32) + self.parts[k][part].astype(F32)
        return at, total.astype(BF16)

    def send_gather(self, u, k):
        order = GATHER_ORDER[u]
        at = (u,) + tuple(
            self.here[axis] if axis in order[k:] else slice(None) for axis in AXES[1:]
        )
        self.copies[u] = self.cp.go(self.whole.at[at], self.whole.at[at], self.peers[order[k]])

    def step(self, u, i):
        if u == "v":
            self.vector(i)
            return
        if i > 0:
            self.copies[u].wait_recv()
        if i == 0:
            self.send_part(u, 0)
        elif i < 4:
            axis = SUM_ORDER[u][i]
            at, total = self.add_part(u, i - 1, **{axis: 1 - self.here[axis]})
            self.grads[at] = total
            self.send_part(u, i)
            at, total = self.add_part(u, i - 1, **{axis: self.here[axis]})
            self.grads[at] = total
        elif i == 4:
            at, total = self.add_part(u, 3)
            self.whole[(u,) + at[2:]] = total
            self.send_gather(u, 0)
        elif i < 7:
            self.send_gather(u, i - 4)
        else:
            self.deliver(u, self.whole.at[u])

    def vector(self, i):
        if i > 0:
            self.copies["v"].wait_recv()
            self.copies["v"].wait_send()
            self.bv[...] += self.bv_in[i - 1]
        if i < 5:
            to = self.peers[("c", *AXES)[i]]
            self.copies["v"] = self.cp.go(self.bv, self.bv_in.at[i], to, keep=False)
        else:
            self.deliver("v", self.bv)


def layer_kernel(
    x_in, cot_in, lens, wj_in, wo_in, wi_in, wd_in,
    *rest,
):
    lines, rest = rest[:13], rest[13:]
    (
    res_out, grad_out, gj_out, go_out, gi_out, gd_out, bv_out,
    wj, wo, wi, wd, feats, cots, ends, normed, q, k, v, vt, bias, pt, scales, mixed,
    sub, fn, handed, tmp, vh, pre, fs, fs_sib, gi_sib, up, gfn, hgr, hg_sib, gmix, do, dqkv,
    result, stat, cols, bv, bv_in, grads, r1, r2, r3, r4, whole,
    vectors, inner_bias, fourth_gain, fourth_bias, *line_refs, lsem, ssem, rsem,
    ) = rest
    R, HD = x_in.shape
    D = 2 * HD
    H = R // 2
    FF = wi.shape[1]
    T = 256
    NT = FF // T
    x = lax.axis_index("section")
    b = lax.axis_index("batch")
    base = (b // GROUP) * GROUP
    z, y, c = (b // 4) % 4, (b // 2) % 2, b % 2
    low, high = z % 2, z // 2

    def dev(x_, z_, y_, c_):
        return (x_, base + z_ * 4 + y_ * 2 + c_)

    sib = dev(x, z, y, 1 - c)
    xp = dev(1 - x, z, y, c)
    xc = dev(1 - x, z, y, 1 - c)
    yp = dev(x, z, 1 - y, c)
    peers = {
        "c": sib, "x": xp, "y": yp,
        "a": dev(x, 2 * high + 1 - low, y, c), "b": dev(x, 2 * (1 - high) + low, y, c),
    }
    home = c == x
    away = c != x
    own = aligned(c * H, 32)
    other = aligned((1 - c) * H, 32)
    cp = Copies(ssem, rsem)
    local_count = [0]

    def local(src, dst):
        copy = pltpu.make_async_copy(src, dst, lsem.at[local_count[0]])
        local_count[0] += 1
        copy.start()
        return copy

    barrier = pltpu.get_barrier_semaphore()
    for peer in (*peers.values(), xc):
        pl.semaphore_signal(barrier, inc=1, device_id=peer, device_id_type=MESH)

    line_refs += [inner_bias, fourth_gain, fourth_bias]
    line_copies = [local(src, dst) for src, dst in zip(lines, line_refs)]
    (
        first_gain, first_bias, query_bias, value_bias, second_gain, second_bias, output_bias,
        third_gain, third_bias, down_bias,
    ) = (vectors.at[i : i + 1] for i in range(10))

    @pl.when(home)
    def _():
        lane = lax.broadcasted_iota(jnp.int32, (1, 8), 1)
        lengths = lens[...].astype(F32)
        for j in range(8):
            end = jnp.sum(jnp.where(lane <= j, lengths, 0.0), axis=1, keepdims=True)
            ends[j : j + 1, :] = jnp.broadcast_to(end, (1, 128))

    pl.semaphore_wait(barrier, 6)

    NC = 3
    RC = R // NC
    c_native = [cp.remote(src, dst.at[x], sib) for src, dst in ((x_in, feats), (cot_in, cots))]
    c_ends = cp.remote(ends, ends, sib)
    c_cross = [
        cp.remote(x_in.at[pl.ds(i * RC, RC)], feats.at[x, pl.ds(i * RC, RC)], xp) for i in range(NC)
    ]
    c_pass = [
        cp.remote(feats.at[1 - x, pl.ds(i * RC, RC)], feats.at[1 - x, pl.ds(i * RC, RC)], sib)
        for i in range(NC)
    ]
    cot_cross = cp.remote(cot_in, cots.at[x], xp)
    cot_pass = cp.remote(cots.at[1 - x], cots.at[1 - x], sib)
    l_native = [
        pltpu.make_async_copy(src, dst.at[x], lsem.at[44 + i])
        for i, (src, dst) in enumerate(((x_in, feats), (cot_in, cots)))
    ]

    @pl.when(away)
    def _():
        c_cross[0].start()
        c_cross[1].start()

    @pl.when(home)
    def _():
        c_native[0].start()
        l_native[0].start()
        c_ends.start()
        l_native[1].start()
        c_native[1].start()
        l_native[0].wait()

    wj_copies = [local(wj_in.at[:, pl.ds(aligned(t * D + c * HD, 128), HD)], wj.at[t]) for t in range(3)]
    wo_copy = local(wo_in, wo)
    wi_copy = local(wi_in, wi)
    wd_copy = local(wd_in, wd)

    @pl.when(away)
    def _():
        c_native[0].wait_recv()
        c_ends.wait_recv()

    for copy in line_copies:
        copy.wait()
    for i in range(10):
        vectors[i : i + 1, :] = line_refs[i][...].reshape(1, D)
    zeros = jnp.zeros((640 - R, HD), BF16)
    for ref in (q, do):
        ref[R:640, :] = zeros

    key_at = lax.broadcasted_iota(jnp.int32, (R, 128), 0).astype(F32)
    key_segment = sum((key_at >= ends[j : j + 1, :]).astype(F32) for j in range(8))
    for j in range(5):
        query_at = (lax.broadcasted_iota(jnp.int32, (1, 128), 1) + j * 128).astype(F32)
        query_segment = sum((query_at >= ends[i : i + 1, :]).astype(F32) for i in range(8))
        allowed = (key_segment == query_segment) & (key_at <= query_at)
        bias[:, j * 128 : (j + 1) * 128] = jnp.where(allowed, 0.0, MASKED).astype(BF16)

    def feature_rows(at, count):
        return jnp.concatenate([feats[0, pl.ds(at, count)], feats[1, pl.ds(at, count)]], 1).astype(F32)

    for copy in wj_copies:
        copy.wait()
    heads_at = aligned(c * HD, 128)
    own_query_bias = query_bias[:, pl.ds(heads_at, HD)]
    own_value_bias = value_bias[:, pl.ds(heads_at, HD)]
    for i in range(NC):

        @pl.when(home)
        def _():
            c_cross[i].wait_recv()
            c_pass[i].start()

        @pl.when(away)
        def _():
            if i == 0:
                c_cross[0].wait_send()
                c_cross[2].start()
            if i == 1:
                c_cross[1].wait_send()
                c_cross[2].wait_send()
                cot_cross.start()
            c_pass[i].wait_recv()

        for at in range(i * RC, (i + 1) * RC, 48):
            vhat, _ = normal(feature_rows(at, 48))
            normed[at : at + 48, :] = (vhat * first_gain[...] + first_bias[...]).astype(BF16)

        rows = normed[i * RC : (i + 1) * RC, :]
        at = pl.ds(i * RC, RC)
        q[at, :] = ((dot(rows, wj[0]) + own_query_bias).astype(BF16) * 0.125).astype(BF16)
        k[at, :] = dot(rows, wj[1]).astype(BF16)
        v[at, :] = (dot(rows, wj[2]) + own_value_bias).astype(BF16)
    vt[:, :R] = v[...].T

    first_half = lax.broadcasted_iota(jnp.int32, (128, 128), 1) < 64

    def split_pair(tile):
        zero = jnp.zeros_like(tile)
        return jnp.concatenate([jnp.where(first_half, tile, zero), jnp.where(first_half, zero, tile)], 0)

    blocks = []
    at = 0
    for j in range(5):
        blocks.append((j, min(128 * (j + 1), R), at))
        at += min(128 * (j + 1), R)
    c_mixed = []
    for pr in range(PAIRS):
        lanes = slice(pr * 128, (pr + 1) * 128)
        for j, nk, at in blocks:
            qs = slice(j * 128, (j + 1) * 128)
            block_bias = bias[:nk, qs].astype(F32)
            scores = dot_t(k[:nk, lanes], split_pair(q[qs, lanes]))
            scores = scores + jnp.concatenate([block_bias, block_bias], 1)
            largest = jnp.max(scores, axis=0, keepdims=True)
            shifted = jnp.exp(scores - largest)
            summed = jnp.sum(shifted, axis=0, keepdims=True)
            scale = 1.0 / summed
            weights = shifted.astype(BF16)
            pt[pr, at : at + nk, :] = weights
            scales[pr * 5 + j] = jnp.broadcast_to(scale, (8, 256))
            out = dot(vt[lanes, :nk], weights) * scale
            out = jnp.concatenate([out[:64, :128], out[64:, 128:]], 0).T
            for half in range(2):
                start, stop = max(j * 128, half * H), min((j + 1) * 128, (half + 1) * H)
                if start < stop:
                    gfn[start - half * H : stop - half * H, half * HD + pr * 128 : half * HD + (pr + 1) * 128] = (
                        out[start - j * 128 : stop - j * 128]
                    )
        there = pl.ds(aligned(c * HD + pr * 128, 128), 128)
        theirs = pl.ds(aligned((1 - c) * HD + pr * 128, 128), 128)
        c_mixed.append(cp.go(gfn.at[:, theirs], mixed.at[:, there], sib, keep=False))
        mixed[:, there] = gfn[:, there]

    kt = vt
    kt[:, :R] = k[...].T

    @pl.when(home)
    def _():
        cot_cross.wait_recv()
        cot_pass.start()
        l_native[1].wait()
        cot_pass.wait_send()

    @pl.when(away)
    def _():
        c_native[1].wait_recv()
        cot_pass.wait_recv()

    for at in range(0, R, 48):
        alive = (lax.broadcasted_iota(jnp.int32, (48, 1), 0) + at).astype(F32) < ends[7:8, 0:1]
        for h in range(2):
            rows = cots[h, pl.ds(at, 48), :].astype(F32)
            cots[h, pl.ds(at, 48), :] = jnp.where(alive, rows, 0.0).astype(BF16)

    up[:, :HD] = cots[0, pl.ds(own, H), :]
    up[:, HD:] = cots[1, pl.ds(own, H), :]

    wo_copy.wait()
    for copy in c_mixed:
        copy.wait_recv()
    own_live = (lax.broadcasted_iota(jnp.int32, (H, 1), 0) + c * H).astype(F32) < ends[7:8, 0:1]

    for i in range(6):
        vhat, _ = normal(mixed[i * 48 : (i + 1) * 48, :])
        sub[pl.ds(own + i * 48, 48), :] = (vhat * second_gain[...] + second_bias[...]).astype(BF16)

    branch = dot(sub[pl.ds(own, H), :], wo[...])
    for i in range(6):
        piece = slice(i * 48, (i + 1) * 48)
        handed[piece, :] = (
            feature_rows(own + i * 48, 48) + (branch[piece] + output_bias[...])
        ).astype(BF16)
        vhat, _ = normal(handed[piece, :].astype(F32))
        fn[pl.ds(own + i * 48, 48), :] = (vhat * third_gain[...] + third_bias[...]).astype(BF16)
    c_sub = cp.go(sub.at[pl.ds(own, H)], sub.at[pl.ds(own, H)], sib)
    c_fn = cp.go(fn.at[pl.ds(own, H)], fn.at[pl.ds(own, H)], sib)

    wi_copy.wait()

    def feed_dot(tile):
        at = pl.ds(aligned(tile * T, T), T)
        tmp[:, at] = dot(fn[pl.ds(own, H), :], wi[:, at])

    def feed_tile(tile, first=False):
        at = pl.ds(aligned(tile * T, T), T)
        for i in range(9):
            piece = slice(i * 32, (i + 1) * 32)
            u = tmp[piece, at] + inner_bias[:, at]
            pre[piece, at] = u.astype(BF16)
            half = 0.5 * u
            act = half + half * jnp.tanh(u * (GELU_C + (GELU_C * GELU_A) * (u * u)))
            tmp[piece, at] = act
            if first:
                near = jnp.sum(act, axis=1, keepdims=True) * (1.0 / T)
                stat[1, piece, :] = jnp.broadcast_to(near, (32, 128))
            near = stat[1, piece, :]
            low, high = act[:, :128] - near, act[:, 128:] - near
            if first:
                stat[0, piece, :] = low + high
                stat[2, piece, :] = low * low + high * high
            else:
                stat[0, piece, :] += low + high
                stat[2, piece, :] += low * low + high * high

    feed_dot(0)
    feed_dot(1)
    feed_tile(0, True)

    for tile in range(1, NT - 1):
        feed_dot(tile + 1)
        feed_tile(tile)

    feed_tile(NT - 1)
    shift = jnp.sum(stat[0], axis=1, keepdims=True) * (1.0 / FF)
    spread = jnp.sum(stat[2], axis=1, keepdims=True) * (1.0 / FF) - shift * shift
    stat[1] = stat[1] + shift
    stat[2] = jnp.broadcast_to(lax.rsqrt(jnp.maximum(spread, 0.0) + EPSILON), (H, 128))

    def feed_norm(block):
        at = pl.ds(aligned(block * HD, HD), HD)
        for i in range(9):
            piece = slice(i * 32, (i + 1) * 32)
            m, s = stat[1, piece, :], stat[2, piece, :]
            vhat = (tmp[piece, at] - jnp.concatenate([m, m, m], 1)) * jnp.concatenate([s, s, s], 1)
            vh[piece, at] = vhat.astype(BF16)
            fs[piece, at] = (vhat * fourth_gain[:, at] + fourth_bias[:, at]).astype(BF16)

    c_fs = []
    for part in range(2):
        for i in range(2):
            feed_norm(4 * i + 2 * (1 - c) + part)
        for i in range(2):
            c_fs.append(
                cp.go(
                    fs.at[:, pl.ds(aligned((4 * i + 2 * (1 - c) + part) * HD, 128), HD)],
                    fs_sib.at[:, (2 * i + part) * HD : (2 * i + part + 1) * HD],
                    sib,
                    keep=False,
                )
            )

    for step in range(4):
        feed_norm((step // 2) * 4 + 2 * c + step % 2)

    deliveries = []

    def deliver(u, total):
        if u == "v":
            deliveries.append((None, local(total, bv_out)))
            return
        rows = (slice(None),) * 4
        if u < 4:
            target = gd_out.at[(c, u // 2) + rows + (slice((u % 2) * HD, (u % 2 + 1) * HD),)]
        elif u < 8:
            target = gi_out.at[rows + (pl.ds(aligned(c * (FF // 2) + (u - 4) * HD, 128), HD),)]
        elif u == 8:
            target = go_out.at[rows + (pl.ds(heads_at, HD),)]
        else:
            target = gj_out.at[rows + (pl.ds(aligned((u - 9) * D + c * HD, 128), HD),)]
        deliveries.append((cp.go(total, target, sib), local(total, target)))

    here = {"x": x, "y": y, "a": low, "b": high}
    sums = Sums(cp, here, peers, grads, (r1, r2, r3, r4), whole, bv, bv_in, deliver)
    schedule = iter(SCHEDULE)

    def pump(mark):
        at, steps = next(schedule)
        assert at == mark
        for u, i in steps:
            sums.step(u, i)


    def cut_rows(unit):
        return unit.astype(BF16).reshape(2, 2, 2, HD // 8, HD)

    def units(first, count, left_own, left_sib, right):
        for i in range(count):
            if first == 0 and i % 2 == 0:
                c_fs[i].wait_recv()
                c_fs[i + 1].wait_recv()
            for h in range(2):
                rows = jnp.concatenate([left_own(i, h), left_sib(i, h)], 0)
                grads[first + i, h] = cut_rows(t_dot(rows, right(i)))
            pump(first + i)

    units(
        0, 4,
        lambda i, h: fs[:, pl.ds(aligned((2 * h + c) * D + (i // 2) * HD, 128), HD)],
        lambda i, h: fs_sib[:, h * D + (i // 2) * HD : h * D + (i // 2 + 1) * HD],
        lambda i: jnp.concatenate([cots[i % 2, pl.ds(own, H), :], cots[i % 2, pl.ds(other, H), :]], 0),
    )

    wd_copy.wait()
    c_result = [
        cp.remote(result.at[0, x], res_out.at[pl.ds(own, H)], sib),
        cp.remote(result.at[0, 1 - x], res_out.at[pl.ds(own, H)], xp),
        cp.remote(result.at[0, 1 - x], res_out.at[pl.ds(own, H)], xc),
        cp.remote(result.at[1, x], grad_out.at[pl.ds(own, H)], sib),
        cp.remote(result.at[1, 1 - x], grad_out.at[pl.ds(own, H)], xp),
        cp.remote(result.at[1, 1 - x], grad_out.at[pl.ds(own, H)], xc),
    ]
    l_result = [
        pltpu.make_async_copy(result.at[i, x], o.at[pl.ds(own, H)], lsem.at[46 + i])
        for i, o in enumerate((res_out, grad_out))
    ]

    def hand_out(i):
        @pl.when(home)
        def _():
            l_result[i].start()
            c_result[3 * i + 1].start()

        @pl.when(away)
        def _():
            c_result[3 * i].start()
            c_result[3 * i + 2].start()

    def handed_out(i):
        @pl.when(home)
        def _():
            l_result[i].wait()
            c_result[3 * i + 1].wait_send()
            c_result[3 * i].wait_recv()

        @pl.when(away)
        def _():
            c_result[3 * i].wait_send()
            c_result[3 * i + 2].wait_send()
            c_result[3 * i + 1].wait_recv()
            c_result[3 * i + 2].wait_recv()

    branch = dot(fs[...], wd[...])
    for i in range(6):
        piece = slice(i * 48, (i + 1) * 48)
        alive = own_live[piece]
        rows = handed[piece, :].astype(F32) + (branch[piece] + down_bias[...])
        rows = jnp.where(alive, rows, 0.0).astype(BF16)
        result[0, 0, piece, :] = rows[:, :HD]
        result[0, 1, piece, :] = rows[:, HD:]
    hand_out(0)
    pump("result")

    stat[0] = jnp.zeros((H, 128), F32)
    stat[1] = jnp.zeros((H, 128), F32)

    def down_dot(tile):
        at = pl.ds(aligned(tile * T, T), T)
        tmp[:, at] = dot_t(up[...], wd[at, :])

    def down_back(tile):
        at = pl.ds(aligned(tile * T, T), T)
        total_gain = jnp.zeros((8, T), F32)
        total_bias = jnp.zeros((8, T), F32)
        for i in range(9):
            piece = slice(i * 32, (i + 1) * 32)
            g = tmp[piece, at]
            vhat = vh[piece, at].astype(F32)
            gv = g * vhat
            total_gain += by8(gv)
            total_bias += by8(g)
            gain = fourth_gain[:, at]
            g, gv = g * gain, gv * gain
            stat[0, piece, :] += g[:, :128] + g[:, 128:]
            stat[1, piece, :] += gv[:, :128] + gv[:, 128:]
        cols[0, tile] = total_gain
        cols[1, tile] = total_bias

    down_dot(0)
    for tile in range(NT):
        if tile + 1 < NT:
            down_dot(tile + 1)
        down_back(tile)
        if tile % 4 == 3:
            pump(f"down_back{tile // 4}")

    for i in range(2):
        mean = jnp.sum(stat[i], axis=1, keepdims=True) * (1.0 / FF)
        stat[i] = jnp.broadcast_to(mean, (H, 128))
    for copy in c_fs:
        copy.wait_send()
    gi = fs

    def inner_back(tile):
        at = pl.ds(aligned(tile * T, T), T)
        total = jnp.zeros((8, T), F32)
        for i in range(9):
            piece = slice(i * 32, (i + 1) * 32)
            m1, m2, s = stat[0, piece, :], stat[1, piece, :], stat[2, piece, :]
            vhat = vh[piece, at].astype(F32)
            grad = tmp[piece, at] * fourth_gain[:, at] - jnp.concatenate([m1, m1], 1)
            grad = (grad - vhat * jnp.concatenate([m2, m2], 1)) * jnp.concatenate([s, s], 1)
            u = pre[piece, at].astype(F32)
            square = u * u
            t = jnp.tanh(u * (GELU_C + (GELU_C * GELU_A) * square))
            half = 0.5 * u
            slope = 0.5 + 0.5 * t + (half - half * t * t) * (
                GELU_C + (3 * GELU_C * GELU_A) * square
            )
            low = (grad * slope).astype(BF16)
            gi[piece, at] = low
            total += by8(low.astype(F32))
        cols[2, tile] = total

    for tile in range(NT):
        inner_back(tile)
        if tile % 6 == 5:
            pump(f"inner_back{tile // 6}")

    c_gi = cp.go(gi.at[:, pl.ds(aligned((1 - c) * (FF // 2), 128), FF // 2)], gi_sib, sib)
    for copy in c_mixed:
        copy.wait_send()
    gfn[...] = dot_t(gi[...], wi[...])
    pump("gfn")

    total_gain = jnp.zeros((8, D), F32)
    total_bias = jnp.zeros((8, D), F32)
    total_out = jnp.zeros((8, D), F32)
    for i in range(6):
        piece = slice(i * 48, (i + 1) * 48)
        vhat, scale = normal(handed[piece, :].astype(F32))
        grad = gfn[piece, :]
        total_gain += by8(grad * vhat)
        total_bias += by8(grad)
        low = (
            up[piece, :].astype(F32) + normal_back(vhat, scale, third_gain[...], grad)
        ).astype(BF16)
        hgr[piece, :] = low
        total_out += by8(low.astype(F32))

    def store_vector(row, total):
        bv[row : row + 1, :] = jnp.sum(total, axis=0, keepdims=True)

    store_vector(6, total_out)
    store_vector(7, total_gain)
    store_vector(8, total_bias)
    c_hg = cp.go(hgr.at[:, pl.ds(aligned((1 - c) * HD, 128), HD)], hg_sib, sib)

    pump("handed")

    gfn[...] = dot_t(hgr[...], wo[...])
    total_gain = jnp.zeros((8, D), F32)
    total_bias = jnp.zeros((8, D), F32)
    for i in range(6):
        piece = slice(i * 48, (i + 1) * 48)
        vhat, scale = normal(mixed[piece, :])
        grad = gfn[piece, :]
        total_gain += by8(grad * vhat)
        total_bias += by8(grad)
        gmix[piece, :] = normal_back(vhat, scale, second_gain[...], grad).astype(BF16)
    store_vector(4, total_gain)
    store_vector(5, total_bias)
    c_gmix = cp.go(
        gmix.at[:, pl.ds(aligned((1 - c) * HD, 128), HD)], do.at[pl.ds(own, H)], sib
    )
    do[pl.ds(own, H), :] = gmix[:, pl.ds(heads_at, HD)]

    pump("mixed")

    c_fn.wait_recv()
    c_gi.wait_recv()

    def fn_rows(at):
        return lambda i, h: fn[pl.ds(at, H), h * HD : (h + 1) * HD]

    units(
        4, 4, fn_rows(own), fn_rows(other),
        lambda i: jnp.concatenate(
            [gi[:, pl.ds(aligned(c * (FF // 2) + i * HD, 128), HD)], gi_sib[:, i * HD : (i + 1) * HD]], 0
        ),
    )
    c_sub.wait_recv()
    c_hg.wait_recv()

    def sub_rows(at):
        return lambda i, h: sub[pl.ds(at, H), h * HD : (h + 1) * HD]

    units(
        8, 1, sub_rows(own), sub_rows(other),
        lambda i: jnp.concatenate([hgr[:, pl.ds(heads_at, HD)], hg_sib[...]], 0),
    )

    c_gmix.wait_recv()
    for pr in range(PAIRS):
        lanes = slice(pr * 128, (pr + 1) * 128)
        for j, nk, at in reversed(blocks):
            qs = slice(j * 128, (j + 1) * 128)
            exact = pt[pr, at : at + nk, :].astype(F32) * scales[pr * 5 + j][:1]
            probs = exact.astype(BF16)
            do_split = split_pair(do[qs, lanes])
            grad_probs = dot_t(v[:nk, lanes], do_split)
            inner_sum = jnp.sum(exact * grad_probs, axis=0, keepdims=True)
            grad_scores = (exact * (grad_probs - inner_sum)).astype(BF16)
            value_part = dot(probs, do_split)
            key_part = dot(grad_scores, split_pair(q[qs, lanes]))
            if j == len(blocks) - 1:
                gfn[:, :128] = value_part[:H]
                gfn[:, 128:256] = value_part[H:]
                gfn[:, 256:384] = key_part[:H]
                gfn[:, 384:512] = key_part[H:]
            else:
                for lane_at, part in ((0, value_part), (256, key_part)):
                    top = min(nk, H)
                    gfn[:top, lane_at : lane_at + 128] += part[:top]
                    if nk > H:
                        gfn[: nk - H, lane_at + 128 : lane_at + 256] += part[H:]
            out = dot(kt[lanes, :nk], grad_scores)
            query_part = jnp.concatenate([out[:64, :128], out[64:, 128:]], 0).T * 0.125
            count = min(128, R - j * 128)
            dqkv[j * 128 : j * 128 + count, lanes] = query_part[:count].astype(BF16)
        for half in range(2):
            rows = slice(half * H, (half + 1) * H)
            dqkv[rows, 2 * HD + pr * 128 : 2 * HD + (pr + 1) * 128] = gfn[
                :, half * 128 : (half + 1) * 128
            ].astype(BF16)
            dqkv[rows, HD + pr * 128 : HD + (pr + 1) * 128] = gfn[
                :, 256 + half * 128 : 256 + (half + 1) * 128
            ].astype(BF16)
        pump(f"heads{pr}")

    for i in range(3):
        for h in range(2):
            grads[9 + i, h] = cut_rows(
                t_dot(normed[:, h * HD : (h + 1) * HD], dqkv[:, i * HD : (i + 1) * HD])
            )
        pump(9 + i)
    bv[2:4, :] = jnp.zeros((2, D), F32)
    for row, at in ((2, 0), (3, 2 * HD)):
        total = jnp.zeros((8, HD), F32)
        for i in range(12):
            total += by8(dqkv[i * 48 : (i + 1) * 48, at : at + HD].astype(F32))
        bv[row : row + 1, pl.ds(heads_at, HD)] = jnp.sum(total, axis=0, keepdims=True)

    for part, at in ((0, other), (1, own)):
        total = jnp.zeros((H, D), F32)
        for i in range(3):
            total += dot_t(dqkv[pl.ds(at, H), i * HD : (i + 1) * HD], wj[i])
        tmp[:, part * D : (part + 1) * D] = total
        if part == 0:
            c_gn = cp.go(tmp.at[:, :D], mixed, sib)
    c_gn.wait_recv()
    pump("joint_back")
    total_gain = jnp.zeros((8, D), F32)
    total_bias = jnp.zeros((8, D), F32)
    total_down = jnp.zeros((8, D), F32)
    for i in range(6):
        piece = slice(i * 48, (i + 1) * 48)
        vhat, scale = normal(feature_rows(own + i * 48, 48))
        grad = tmp[piece, D : 2 * D] + mixed[piece, :]
        total_gain += by8(grad * vhat)
        total_bias += by8(grad)
        total_down += by8(up[piece, :].astype(F32))
        rows = (
            hgr[piece, :].astype(F32) + normal_back(vhat, scale, first_gain[...], grad)
        ).astype(BF16)
        result[1, 0, piece, :] = rows[:, :HD]
        result[1, 1, piece, :] = rows[:, HD:]
    hand_out(1)
    store_vector(0, total_gain)
    store_vector(1, total_bias)
    store_vector(9, total_down)
    for kind, row in ((2, 10), (0, 14), (1, 18)):
        for tile in range(NT):
            bv[row + tile // 3 : row + tile // 3 + 1, (tile % 3) * T : (tile % 3 + 1) * T] = jnp.sum(
                cols[kind, tile], axis=0, keepdims=True
            )
    bv[22:24, :] = jnp.zeros((2, D), F32)

    pump("end")

    @pl.when(home)
    def _():
        for copy in c_native + [c_ends] + c_pass:
            copy.wait_send()

    @pl.when(away)
    def _():
        cot_cross.wait_send()

    handed_out(0)
    handed_out(1)
    for copy, here in deliveries:
        if copy is not None:
            copy.wait_recv()
        here.wait()
    cp.drain()


def finish_kernel(gj, go, gi, gd, bv, res, grad, oj, oo, oi, od, *rest):
    *vectors, res_out, grad_out = rest

    @pl.when(pl.program_id(0) == 0)
    def _():
        x = lax.axis_index("section")
        HD = oo.shape[1] // 2
        at = pl.ds(aligned(x * HD, 128), HD)
        for row in range(10):
            vectors[row][...] = bv[row : row + 1, at].reshape(HD)
        for i in range(3):
            row = 10 + 4 * i
            halves = [jnp.concatenate([bv[j : j + 1, :], bv[j + 1 : j + 2, :]], 1) for j in (row, row + 2)]
            vectors[10 + i][...] = jnp.where(x == 0, *halves).reshape(4 * HD)

    oj[...] = gj[...].astype(F32)
    oo[...] = go[...].astype(F32)
    oi[...] = gi[...].astype(F32)
    od[...] = gd[...].astype(F32)

    res_out[...] = res[...]
    grad_out[...] = grad[...]


def per_device(
    inputs, seq_lengths, cotangent,
    first_gain, first_bias, joint_weight, query_bias, value_bias, second_gain, second_bias,
    output_weight, output_bias, third_gain, third_bias, inner_weight, inner_bias,
    fourth_gain, fourth_bias, down_weight, down_bias,
):
    R, HD = inputs.shape
    D, H, FF = 2 * HD, R // 2, inner_weight.shape[1]
    hbm = pl.BlockSpec(memory_space=pl.ANY)
    vmem = pl.BlockSpec(memory_space=pltpu.VMEM)
    lines = (
        first_gain, first_bias, query_bias, value_bias, second_gain, second_bias, output_bias,
        third_gain, third_bias, down_bias,
    )
    lines += tuple(m.reshape(1, -1) for m in (inner_bias, fourth_gain, fourth_bias))
    V = pltpu.VMEM
    scratch = [
        V((3, D, HD), BF16), V((D, D), BF16), V((D, FF), BF16), V((FF, D), BF16),
        V((2, R, HD), BF16), V((2, R, HD), BF16), V((8, 128), F32), V((R, D), BF16),
        V((640, HD), BF16), V((R, HD), BF16), V((R, HD), BF16),
        V((HD, 640), BF16), V((R, 640), BF16),
        V((PAIRS, 128 * 10 + R, 256), BF16), V((PAIRS * 5, 8, 256), F32),
        V((H, D), F32),
        V((R, D), BF16), V((R, D), BF16), V((H, D), BF16),
        V((H, FF), F32), V((H, FF), BF16), V((H, FF), BF16),
        V((H, FF), BF16), V((H, FF // 2), BF16), V((H, FF // 2), BF16),
        V((H, D), BF16), V((H, D), F32), V((H, D), BF16), V((H, HD), BF16),
        V((H, D), BF16), V((640, HD), BF16), V((R, 3 * HD), BF16),
        V((2, 2, H, HD), BF16), V((3, H, 128), F32),
        V((3, FF // 256, 8, 256), F32), V((24, D), F32), V((5, 24, D), F32),
        V((UNITS, 2, 2, 2, 2, HD // 8, HD), BF16),
        V((UNITS, 2, 2, 2, HD // 8, HD), BF16), V((UNITS, 2, 2, HD // 8, HD), BF16),
        V((UNITS, 2, HD // 8, HD), BF16), V((UNITS, HD // 8, HD), BF16),
        V((UNITS, 2, 2, 2, HD // 8, HD), BF16),
        V((10, D), F32), *[V((1, FF), F32)] * 3, *[V((D,), F32)] * 10,
        pltpu.SemaphoreType.DMA((48,)), pltpu.SemaphoreType.DMA((200,)), pltpu.SemaphoreType.DMA((200,)),
    ]
    shape = jax.ShapeDtypeStruct
    result, input_grad, gj, go, gi, gd, bv = pl.pallas_call(
        layer_kernel,
        out_shape=[
            shape((R, HD), BF16), shape((R, HD), BF16),
            *(shape((2, 2, 2, HD // 8, n), BF16) for n in (3 * D, D, FF)),
            shape((2, 2, 2, 2, 2, HD // 8, D), BF16), shape((24, D), F32),
        ],
        in_specs=[hbm, hbm, vmem, hbm, hbm, hbm, hbm] + [hbm] * 13,
        out_specs=[hbm] * 7,
        scratch_shapes=scratch,
        compiler_params=pltpu.CompilerParams(
            collective_id=0, has_side_effects=True, vmem_limit_bytes=66_000_000
        ),
        cost_estimate=pl.CostEstimate(flops=16 * 10**9, bytes_accessed=25 * 10**6, transcendentals=4 * 10**6),
    )(inputs, cotangent, seq_lengths, joint_weight, output_weight, inner_weight, down_weight, *lines)
    steps = 2
    wide = [(HD, 3 * D), (HD, D), (HD, FF), (FF // 2, D)]
    gj, go, gi, gd = (m.reshape(s) for m, s in zip((gj, go, gi, gd), wide))

    def block(rows, columns):
        return pl.BlockSpec((rows // steps, columns), lambda i: (i, 0))

    small = [(HD,)] * 10 + [(FF // 2,)] * 3
    groups = lax.axis_size("batch") // GROUP
    if groups > 1:
        peers = [[r + GROUP * g for g in range(groups)] for r in range(GROUP)]
        gj, go, gi, gd, bv = lax.psum(
            tuple(m.astype(F32) for m in (gj, go, gi, gd, bv)), "batch", axis_index_groups=peers
        )
    outs = pl.pallas_call(
        finish_kernel,
        grid=(steps,),
        out_shape=[shape(s, F32) for s in wide + small] + [shape((R, HD), BF16)] * 2,
        in_specs=[block(*s) for s in wide] + [pl.BlockSpec((24, D), lambda i: (0, 0))] + [block(R, HD)] * 2,
        out_specs=[block(*s) for s in wide] + [pl.BlockSpec(s, lambda i: (0,)) for s in small] + [block(R, HD)] * 2,
        compiler_params=pltpu.CompilerParams(vmem_limit_bytes=66_000_000),
    )(gj, go, gi, gd, bv, result, input_grad)
    result, input_grad = outs[-2:]
    dj, dout, di, dd = outs[:4]
    fg, fb, qb, vb, sg, sb, ob, tg, tb, db, ib, hg, hb = outs[4:-2]
    return (
        result, input_grad, fg, fb, dj, qb, vb, sg, sb, dout, ob, tg, tb, di, ib, hg, hb, dd, db,
    )


def solution(mesh):
    wide = P("section", None)
    line = P("section")
    return jax.shard_map(
        per_device,
        mesh=mesh,
        in_specs=(P("batch", "section"), P("batch", None), P("batch", "section")) + (P(),) * 17,
        out_specs=(
            P("batch", "section"), P("batch", "section"), line, line, wide, line, line, line, line,
            wide, line, line, line, wide, line, line, line, wide, line,
        ),
        check_vma=False,
    )
```
